128 devices in a mesh: grp: 4 (over y_hi, core), resp: 32 (over y_lo, z, x).
Axes of the slice: x: 4, y: 4 (y_hi: 2, y_lo: 2; y = y_hi * 2 + y_lo), z: 4, core: 2. Of those that a mesh axis runs over, the one named last changes fastest.
Arguments:
- roll_query: bfloat16 [16384, 8192], P(('grp', 'resp')), may hold values from -8 to 8
- roll_keyval: bfloat16 [16384, 2048], P(('grp', 'resp')), may hold values from -6 to 6
- roll_grad: bfloat16 [16384, 8192], P(('grp', 'resp')), may hold values from -6 to 6
- prompt_keyval: bfloat16 [4, 2048, 2048], P('grp', 'resp'), may hold values from -6 to 6
- lengths: int32 [4, 64], P('grp', 'resp'), may hold values from 1 to 64, as said below
- send_rows: int32 [4, 32, 128], P('grp', 'resp'), may hold values from 0 to 127, each once within a row
- land_rows: int32 [4, 32, 128], P('grp', 'resp'), may hold values from 0 to 127, each once within a row
Outputs:
- attn_out: bfloat16 [16384, 8192], P(('grp', 'resp'))
- query_grad: bfloat16 [16384, 8192], P(('grp', 'resp'))
- pair_grad: bfloat16 [16384, 2048], P(('grp', 'resp'))
- prompt_grad: float32 [4, 2048, 2048], P('grp', 'resp')
The draws below stay inside these ranges and needn't reach their ends.
Inputs may be any that keep to these rules, and one draw needn't show every extreme that they name: `lengths`: each response has 1 to 64 tokens; some response has exactly 64. `send_rows`: each device's list is a permutation of its 128 rows; entries g * 32 to g * 32 + 31 go to grp index g. `land_rows`: each device's list is a permutation; entry f names received row f % 32 from grp index f // 32.
All inputs are finite; a program needn't handle non-finite values.
Results may differ from the reference program's by a relative error of at most 0.012.
The reference program's roundings to bfloat16 on the way count: a program that leaves them out, or rounds other values in their place, can miss the bound.
Values may be sent and summed in bfloat16 or wider, within the bound.
No kernel may reach another device: no remote copies, remote signals or barrier semaphores. Data moves between devices by JAX's collectives and lax.ppermute only.
A program may use at most 192 MiB of HBM per device.

```python
import math
import jax
import jax.numpy as jnp
from jax import lax

HEADS = 64
KV_HEADS = 8
HEAD_DIM = 128
RESP_LEN = 64
PROMPT_LEN = 2048
SLOTS = 2
ROWS = 128
QW = 8192
KW = 1024
TOTAL_ROWS = 16384
N_GRP = 4
N_RESP = 32


def draw_roll_query(key, part):
    key = jax.random.fold_in(key, 11)
    total_rows = N_GRP * N_RESP * ROWS
    values = jnp.clip(1.5 * jax.random.normal(key, (total_rows, QW), jnp.float32), -8.0, 8.0)
    return values.astype(jnp.bfloat16)


def draw_prompt_keyval(key, part):
    key = jax.random.fold_in(key, 12)
    shape = (N_GRP, PROMPT_LEN, 2 * KW)
    values = jnp.clip(jax.random.normal(key, shape, jnp.float32), -6.0, 6.0)
    return values.astype(jnp.bfloat16)


def draw_lengths(key, part):
    key = jax.random.fold_in(key, 5)
    first, second = jax.random.split(key)
    shape = (N_GRP, N_RESP * SLOTS)
    left = jax.random.randint(first, shape, 0, RESP_LEN)
    right = jax.random.randint(second, shape, 0, RESP_LEN)
    counts = RESP_LEN - left * right // RESP_LEN
    counts = counts.at[:, 0].set(RESP_LEN)
    return counts.astype(jnp.int32)


def steps_of(stream_key, extent, pieces, least, top_value):
    factor_of = 1.0
    for dim, shards_of in pieces:
        steps = jax.random.uniform(jax.random.fold_in(jax.random.fold_in(stream_key, 6), dim), (shards_of,), jnp.float32, least / len(pieces), top_value / len(pieces))
        factor_of = factor_of * jnp.repeat(jnp.exp(steps), extent[dim] // shards_of).reshape((-1,) + (1,) * (len(extent) - 1 - dim))
    return factor_of


def bell_draw(stream_key, extent, scale, most, shards=(), kind=jnp.bfloat16):
    drawn = scale * jax.random.normal(stream_key, extent, jnp.float32)
    if shards:
        drawn = drawn * steps_of(stream_key, extent, shards, -0.22, 0.18)
    return jnp.clip(drawn, -most, most).astype(kind)


def setup_inputs(seed: int = 0) -> dict:
    keys = jax.random.split(jax.random.key(seed), 8)
    return {
        "roll_query": draw_roll_query(jax.random.fold_in(keys[7], 71), 0),
        "roll_keyval": bell_draw(keys[1], (TOTAL_ROWS, 2 * KW), 1.0, 6.0, ((0, 128),)),
        "roll_grad": bell_draw(keys[2], (TOTAL_ROWS, QW), 1.0, 6.0, ((0, 128),)),
        "prompt_keyval": draw_prompt_keyval(jax.random.fold_in(keys[7], 71), 0),
        "lengths": draw_lengths(jax.random.fold_in(keys[7], 71), 0),
        "send_rows": jax.vmap(lambda own: jax.random.permutation(own, ROWS))(jax.random.split(keys[5], N_GRP * N_RESP)).reshape((N_GRP, N_RESP, ROWS)).astype(jnp.int32),
        "land_rows": jax.vmap(lambda own: jax.random.permutation(own, ROWS))(jax.random.split(keys[6], N_GRP * N_RESP)).reshape((N_GRP, N_RESP, ROWS)).astype(jnp.int32),
    }


def take_head(array, index, axis):
    return lax.dynamic_index_in_dim(array, index, axis, keepdims=False)

def to_bf16_f32(array):
    return lax.optimization_barrier(array.astype(jnp.bfloat16)).astype(jnp.float32)

def head_pass(query, grad_out, own_key, own_value, prompt_key, prompt_value, live):
    rows, group, width = query.shape
    slots = rows // RESP_LEN
    scale = 1.0 / math.sqrt(width)
    query = query.astype(jnp.float32)
    grad_out = grad_out.astype(jnp.float32)
    key_slot = own_key.astype(jnp.float32).reshape(slots, RESP_LEN, width)
    value_slot = own_value.astype(jnp.float32).reshape(slots, RESP_LEN, width)
    prompt_key = prompt_key.astype(jnp.float32)
    prompt_value = prompt_value.astype(jnp.float32)
    query_slot = query.reshape(slots, RESP_LEN, group, width)
    grad_slot = grad_out.reshape(slots, RESP_LEN, group, width)
    score_far = jnp.einsum('rgd,pd->grp', query, prompt_key) * scale
    score_near = jnp.einsum('stgd,sud->gstu', query_slot, key_slot) * scale
    causal = jnp.arange(RESP_LEN)[None, :] <= jnp.arange(RESP_LEN)[:, None]
    score_near = jnp.where(causal, score_near, -jnp.inf)
    largest = jnp.maximum(lax.optimization_barrier(jnp.max(score_far, axis=-1)), lax.optimization_barrier(jnp.max(score_near, axis=-1)).reshape(group, rows))
    exp_far = jnp.exp(score_far - largest[:, :, None])
    exp_near = jnp.exp(score_near - largest.reshape(group, slots, RESP_LEN)[..., None])
    total = lax.optimization_barrier(jnp.sum(exp_far, axis=-1)) + lax.optimization_barrier(jnp.sum(exp_near, axis=-1)).reshape(group, rows)
    factor = live.astype(jnp.float32)[None, :] / total
    weight_far = exp_far * factor[:, :, None]
    weight_near = exp_near * factor.reshape(group, slots, RESP_LEN)[..., None]
    rounded_far = to_bf16_f32(weight_far)
    rounded_near = to_bf16_f32(weight_near)
    attended = jnp.einsum('grp,pd->rgd', rounded_far, prompt_value)
    attended = attended + jnp.einsum('gstu,sud->stgd', rounded_near, value_slot).reshape(rows, group, width)
    attended = attended.astype(jnp.bfloat16)
    delta = lax.optimization_barrier(jnp.sum(grad_out * attended.astype(jnp.float32), axis=-1)).T
    dot_far = jnp.einsum('rgd,pd->grp', grad_out, prompt_value)
    dot_near = jnp.einsum('stgd,sud->gstu', grad_slot, value_slot)
    slope_far = to_bf16_f32(weight_far * (dot_far - delta[:, :, None]) * scale)
    slope_near = to_bf16_f32(weight_near * (dot_near - delta.reshape(group, slots, RESP_LEN)[..., None]) * scale)
    query_grad = jnp.einsum('grp,pd->rgd', slope_far, prompt_key)
    query_grad = query_grad + jnp.einsum('gstu,sud->stgd', slope_near, key_slot).reshape(rows, group, width)
    key_grad = jnp.einsum('gstu,stgd->sud', slope_near, query_slot).reshape(rows, width)
    value_grad = jnp.einsum('gstu,stgd->sud', rounded_near, grad_slot).reshape(rows, width)
    prompt_key_grad = jnp.einsum('grp,rgd->pd', slope_far, query)
    prompt_value_grad = jnp.einsum('grp,rgd->pd', rounded_far, grad_out)
    return (attended, query_grad.astype(jnp.bfloat16), key_grad.astype(jnp.bfloat16), value_grad.astype(jnp.bfloat16), prompt_key_grad, prompt_value_grad)

def device_pass(query, keyval, grad_out, lens, prompt):
    rows = query.shape[0]
    group = HEADS // KV_HEADS
    query4 = query.reshape(rows, KV_HEADS, group, HEAD_DIM)
    grad4 = grad_out.reshape(rows, KV_HEADS, group, HEAD_DIM)
    pair4 = keyval.reshape(rows, 2, KV_HEADS, HEAD_DIM)
    prompt4 = prompt.reshape(prompt.shape[0], 2, KV_HEADS, HEAD_DIM)
    live = jnp.arange(rows, dtype=jnp.int32) % RESP_LEN < jnp.repeat(lens, RESP_LEN, total_repeat_length=rows)

    def one_head(index):
        return head_pass(take_head(query4, index, 1), take_head(grad4, index, 1), take_head(pair4[:, 0], index, 1), take_head(pair4[:, 1], index, 1), take_head(prompt4[:, 0], index, 1), take_head(prompt4[:, 1], index, 1), live)
    attended, query_grad, key_grad, value_grad, prompt_key_grad, prompt_value_grad = lax.map(one_head, jnp.arange(KV_HEADS, dtype=jnp.int32))
    attended = attended.transpose(1, 0, 2, 3).reshape(rows, HEADS * HEAD_DIM)
    query_grad = query_grad.transpose(1, 0, 2, 3).reshape(rows, HEADS * HEAD_DIM)
    pair_grad = jnp.stack([key_grad, value_grad], 0).transpose(2, 0, 1, 3).reshape(rows, 2 * KV_HEADS * HEAD_DIM)
    prompt_grad = jnp.stack([prompt_key_grad, prompt_value_grad], 0).transpose(2, 0, 1, 3)
    prompt_grad = prompt_grad.reshape(prompt.shape[0], 2 * KV_HEADS * HEAD_DIM)
    return (attended, query_grad, pair_grad, prompt_grad)

def reference(roll_query, roll_keyval, roll_grad, prompt_keyval, lengths, send_rows, land_rows):
    cap = ROWS // N_GRP
    group_index = jnp.arange(N_GRP, dtype=jnp.int32)[:, None, None]
    column_index = jnp.arange(N_RESP, dtype=jnp.int32)[None, :, None]
    source = land_rows // cap
    within = land_rows % cap
    picked = send_rows[source, column_index, group_index * cap + within]
    flat = ((source * N_RESP + column_index) * ROWS + picked).reshape(-1).astype(jnp.int32)
    query = roll_query[flat].reshape(N_GRP, N_RESP, ROWS, roll_query.shape[1])
    keyval = roll_keyval[flat].reshape(N_GRP, N_RESP, ROWS, roll_keyval.shape[1])
    grad_out = roll_grad[flat].reshape(N_GRP, N_RESP, ROWS, roll_grad.shape[1])
    lens = lengths.reshape(N_GRP, N_RESP, SLOTS)

    def per_group(items):
        query_group, keyval_group, grad_group, lens_group, prompt_group = items

        def per_device(summed, piece):
            attended, query_grad, pair_grad, prompt_term = device_pass(piece[0], piece[1], piece[2], piece[3], prompt_group)
            return (summed + prompt_term, (attended, query_grad, pair_grad))
        start = jnp.zeros(prompt_group.shape, jnp.float32)
        summed, outputs = lax.scan(per_device, start, (query_group, keyval_group, grad_group, lens_group))
        return (outputs[0], outputs[1], outputs[2], summed)
    attended, query_grad, pair_grad, prompt_grad = lax.map(per_group, (query, keyval, grad_out, lens, prompt_keyval))
    return (attended.reshape(-1, roll_query.shape[1]), query_grad.reshape(-1, roll_query.shape[1]), pair_grad.reshape(-1, roll_keyval.shape[1]), prompt_grad)
```

```python
import functools
import math

import jax
import jax.numpy as jnp
from jax import lax
from jax.experimental import pallas as pl
from jax.experimental.pallas import tpu as pltpu
from jax.sharding import Mesh, PartitionSpec as P

KV_HEADS = 8
GROUP = 8
HD = 128
ROWS = 128
RESP_LEN = 64
NPOS = 2048
OWN = 64
META = 16
SCALE = 1.0 / math.sqrt(HD)
EXP_SCALE = SCALE * math.log2(math.e)
F32 = jnp.float32
BF = jnp.bfloat16
NN = ((1,), (0,))
NT = ((1,), (1,))

CHUNKS = (4, 4)
TILE_ROWS = 512
POS_BLOCK = 512
VMEM = 56 * 1024 * 1024


def dot(a, b, dims):
    return lax.dot_general(a, b, (dims, ((), ())), preferred_element_type=F32)


def full(shape):
    return pl.BlockSpec(shape, lambda i: (0,) * len(shape))


def params():
    return pltpu.CompilerParams(dimension_semantics=("arbitrary",), vmem_limit_bytes=VMEM)


def one_hot_rows(picks):
    chosen = lax.broadcasted_iota(jnp.int32, (ROWS, ROWS), 0) == picks
    return jnp.transpose(chosen.astype(F32)).astype(BF)


def pack_prompt_kernel(key, value, land, lens, out):
    block = key.shape[0]
    lane = lax.broadcasted_iota(jnp.int32, (META, HD), 1)
    counts = jnp.where(lane == 0, lens[:, 0:1], lens[:, 1:2]).astype(F32).astype(BF)
    rows = jnp.broadcast_to(land[0], (META, HD)).astype(F32).astype(BF)
    for copy in range(4):
        out[0, copy, :block, :HD] = key[...]
        out[0, copy, :block, HD:] = value[...]
        out[0, copy, block:, :HD] = rows
        out[0, copy, block:, HD:] = counts


def pack_prompt(prompt, land, lens):
    return pl.pallas_call(
        pack_prompt_kernel,
        grid=(KV_HEADS,),
        in_specs=[
            pl.BlockSpec((OWN, HD), lambda i: (0, i)),
            pl.BlockSpec((OWN, HD), lambda i: (0, KV_HEADS + i)),
            full((1, 1, ROWS)),
            full((1, 2)),
        ],
        out_specs=pl.BlockSpec((1, 4, OWN + META, 2 * HD), lambda i: (i, 0, 0, 0)),
        out_shape=jax.ShapeDtypeStruct((KV_HEADS, 4, OWN + META, 2 * HD), BF),
        compiler_params=params(),
        name="pack_prompt",
    )(prompt, prompt, land, lens)


def pack_rows_kernel(width, send, *refs):
    out = refs[-1]
    order = one_hot_rows(send[0])
    at = 0
    for ref in refs[:-1]:
        wide = ref.shape[1]
        moved = dot(order, ref[...], NN).astype(BF)
        out[:, 0, :, at : at + wide] = moved.reshape(4, 32, wide)
        at += wide


def pack_rows(heads, start, with_pair, query, grad, pair, send):
    wide = heads * HD
    per = GROUP // heads
    first = start // heads
    specs = [full((1, 1, ROWS))]
    specs += [pl.BlockSpec((ROWS, wide), lambda i: (0, i * per + first))] * 2
    arrays = [send, query, grad]
    width = 2 * wide
    if with_pair:
        specs += [
            pl.BlockSpec((ROWS, HD), lambda i: (0, i)),
            pl.BlockSpec((ROWS, HD), lambda i: (0, KV_HEADS + i)),
        ]
        arrays += [pair, pair]
        width += 2 * HD
    return pl.pallas_call(
        functools.partial(pack_rows_kernel, width),
        grid=(KV_HEADS,),
        in_specs=specs,
        out_specs=pl.BlockSpec((4, 1, 32, width), lambda i: (0, i, 0, 0)),
        out_shape=jax.ShapeDtypeStruct((4, KV_HEADS, 32, width), BF),
        compiler_params=params(),
        name="pack_rows",
    )(*arrays)


def attend_kernel(heads, first, last, tile, *refs):
    refs = list(refs)
    where_x, prompt, rows_ref = refs[:3]
    refs = refs[3:]
    if not first:
        pair_ref, far_in, near_in = refs[:3]
        refs = refs[3:]
    out, far_out = refs[:2]
    refs = refs[2:]
    if not last:
        near_out = refs[0]
        refs = refs[1:]
    key_far, value_far, expo, rounded, key_sum, value_sum = refs
    step = pl.program_id(0)
    wide = heads * HD

    @pl.when(step == 0)
    def _():
        key_far[...] = prompt[:, :OWN, :HD].reshape(NPOS, HD)
        value_far[...] = prompt[:, :OWN, HD:].reshape(NPOS, HD)
        if first:
            key_sum[...] = jnp.zeros_like(key_sum)
            value_sum[...] = jnp.zeros_like(value_sum)
        else:
            key_sum[...] = far_in[0]
            value_sum[...] = far_in[1]

    meta = prompt[step * 4 + where_x[0], OWN:, :].astype(F32)
    order = one_hot_rows(meta[0:1, :HD].astype(jnp.int32))
    moved = dot(order, rows_ref[:, 0].reshape(ROWS, -1), NN).astype(BF)
    if first:
        pair = moved[:, 2 * wide :]
    else:
        pair = dot(order, pair_ref[:, 0].reshape(ROWS, -1), NN).astype(BF)
    key_near = pair[:, :HD]
    value_near = pair[:, HD:]

    row = lax.broadcasted_iota(jnp.int32, (ROWS, 1), 0)
    count = jnp.where(row < RESP_LEN, meta[0:1, HD : HD + 1], meta[0:1, HD + 1 : HD + 2] + RESP_LEN)
    live = (row.astype(F32) < count).astype(F32)
    at = lax.broadcasted_iota(jnp.int32, (ROWS, ROWS), 0)
    of = lax.broadcasted_iota(jnp.int32, (ROWS, ROWS), 1)
    seen = (of <= at) & ((of // RESP_LEN) == (at // RESP_LEN))
    hide = jnp.where(seen, 0.0, -1e30).astype(F32)
    per = tile // ROWS
    live = jnp.concatenate([live] * per, 0)
    hide = jnp.concatenate([hide] * per, 0)
    key_own = jnp.zeros((HD, ROWS), F32)
    value_own = jnp.zeros((HD, ROWS), F32)
    blocks = [slice(b, b + POS_BLOCK) for b in range(0, NPOS, POS_BLOCK)]
    lanes = [slice(j, j + HD) for j in range(0, POS_BLOCK, HD)]
    for part in range(heads // per):
        cols = [slice((part * per + a) * HD, (part * per + a + 1) * HD) for a in range(per)]
        query = jnp.concatenate([moved[:, c] for c in cols], 0)
        grad = jnp.concatenate([moved[:, wide + c.start : wide + c.stop] for c in cols], 0)
        query_t = query.T
        grad_t = grad.T
        score_near = dot(query, key_near, NT) + hide
        largest = score_near
        for b in blocks:
            score = dot(query, key_far[b], NT)
            expo[:, b] = score
            for j in lanes:
                largest = jnp.maximum(largest, score[:, j])
        shift = jnp.max(largest, axis=1, keepdims=True) * EXP_SCALE
        exp_near = jnp.exp2(score_near * EXP_SCALE - shift)
        total = exp_near
        for b in blocks:
            value = jnp.exp2(expo[:, b] * EXP_SCALE - shift)
            expo[:, b] = value
            for j in lanes:
                total = total + value[:, j]
        factor = live / jnp.sum(total, axis=1, keepdims=True)
        rounded_near = (exp_near * factor).astype(BF)
        attended = dot(rounded_near, value_near, NN)
        for b in blocks:
            weight = (expo[:, b] * factor).astype(BF)
            rounded[:, b] = weight
            attended = attended + dot(weight, value_far[b], NN)
        attended = attended.astype(BF)
        delta = jnp.sum(grad.astype(F32) * attended.astype(F32), axis=1, keepdims=True)
        scaled = factor * SCALE
        slope = (exp_near * scaled * (dot(grad, value_near, NT) - delta)).astype(BF)
        query_grad = dot(slope, key_near, NN)
        key_own = key_own + dot(query_t, slope, NN)
        value_own = value_own + dot(grad_t, rounded_near, NN)
        for b in blocks:
            slope = (expo[:, b] * scaled * (dot(grad, value_far[b], NT) - delta)).astype(BF)
            query_grad = query_grad + dot(slope, key_far[b], NN)
            key_sum[:, b] += dot(query_t, slope, NN)
            value_sum[:, b] += dot(grad_t, rounded[:, b], NN)
        query_grad = query_grad.astype(BF)
        for a, c in enumerate(cols):
            own = slice(a * ROWS, (a + 1) * ROWS)
            out[0, :, c] = attended[own]
            out[0, :, wide + c.start : wide + c.stop] = query_grad[own]
    if not first:
        key_own = key_own + near_in[0, 0]
        value_own = value_own + near_in[0, 1]
    if last:
        out[0, :, 2 * wide : 2 * wide + HD] = key_own.T.astype(BF)
        out[0, :, 2 * wide + HD :] = value_own.T.astype(BF)
    else:
        near_out[0, 0] = key_own
        near_out[0, 1] = value_own

    @pl.when(step == KV_HEADS - 1)
    def _():
        if last:
            far_out[:, :, :HD] = key_sum[...].T.astype(BF).reshape(NPOS // OWN, OWN, HD)
            far_out[:, :, HD:] = value_sum[...].T.astype(BF).reshape(NPOS // OWN, OWN, HD)
        else:
            far_out[0] = key_sum[...]
            far_out[1] = value_sum[...]


def attend(heads, first, last, where_x, prompt, rows, pair_rows, pair_lane, far, near):
    tile = min(TILE_ROWS, heads * ROWS)
    wide = 2 * heads * HD
    width_in = wide + (2 * HD if first else 0)
    width_out = wide + (2 * HD if last else 0)
    near_spec = pl.BlockSpec((1, 2, HD, ROWS), lambda i: (i, 0, 0, 0))
    arrays = [where_x, prompt, rows]
    specs = [
        pl.BlockSpec(memory_space=pltpu.SMEM),
        full((NPOS // OWN, OWN + META, 2 * HD)),
        pl.BlockSpec((4, 1, 32, width_in), lambda i: (0, i, 0, 0)),
    ]
    if not first:
        arrays += [pair_rows, far, near]
        specs += [
            pl.BlockSpec((4, 1, 32, 2 * HD), lambda i: (0, i, 0, pair_lane)),
            full((2, HD, NPOS)),
            near_spec,
        ]
    shapes = [jax.ShapeDtypeStruct((KV_HEADS, ROWS, width_out), BF)]
    out_specs = [pl.BlockSpec((1, ROWS, width_out), lambda i: (i, 0, 0))]
    if last:
        shapes.append(jax.ShapeDtypeStruct((NPOS // OWN, OWN, 2 * HD), BF))
        out_specs.append(full((NPOS // OWN, OWN, 2 * HD)))
    else:
        shapes.append(jax.ShapeDtypeStruct((2, HD, NPOS), F32))
        out_specs.append(full((2, HD, NPOS)))
        shapes.append(jax.ShapeDtypeStruct((KV_HEADS, 2, HD, ROWS), F32))
        out_specs.append(near_spec)
    return pl.pallas_call(
        functools.partial(attend_kernel, heads, first, last, tile),
        grid=(KV_HEADS,),
        in_specs=specs,
        out_specs=out_specs,
        out_shape=shapes,
        scratch_shapes=[
            pltpu.VMEM((NPOS, HD), BF),
            pltpu.VMEM((NPOS, HD), BF),
            pltpu.VMEM((tile, NPOS), F32),
            pltpu.VMEM((tile, NPOS), BF),
            pltpu.VMEM((HD, NPOS), F32),
            pltpu.VMEM((HD, NPOS), F32),
        ],
        compiler_params=params(),
        name="attend",
    )(*arrays)


def unpack_kernel(chunks, *refs):
    attn_out, query_grad, pair_grad = refs[-3:]
    step = pl.program_id(0)
    at = 0
    for heads, ref in zip(chunks, refs[:-3]):
        wide = heads * HD
        attn_out[:, at : at + wide] = ref[0, :, :wide]
        query_grad[:, at : at + wide] = ref[0, :, wide : 2 * wide]
        at += wide
    key_at = pl.ds(pl.multiple_of(step * HD, HD), HD)
    value_at = pl.ds(pl.multiple_of((KV_HEADS + step) * HD, HD), HD)
    pair_grad[:, key_at] = ref[0, :, 2 * wide : 2 * wide + HD]
    pair_grad[:, value_at] = ref[0, :, 2 * wide + HD :]


def unpack(chunks, arrays):
    wide = GROUP * HD
    return pl.pallas_call(
        functools.partial(unpack_kernel, chunks),
        grid=(KV_HEADS,),
        in_specs=[pl.BlockSpec((1,) + a.shape[1:], lambda i: (i, 0, 0)) for a in arrays],
        out_specs=[
            pl.BlockSpec((ROWS, wide), lambda i: (0, i)),
            pl.BlockSpec((ROWS, wide), lambda i: (0, i)),
            full((ROWS, 2 * KV_HEADS * HD)),
        ],
        out_shape=[
            jax.ShapeDtypeStruct((ROWS, KV_HEADS * wide), BF),
            jax.ShapeDtypeStruct((ROWS, KV_HEADS * wide), BF),
            jax.ShapeDtypeStruct((ROWS, 2 * KV_HEADS * HD), BF),
        ],
        compiler_params=params(),
        name="unpack",
    )(*arrays)


def add_terms_kernel(terms, out):
    step = pl.program_id(0)
    summed = terms[0].astype(F32)
    for i in range(1, 4):
        summed = summed + terms[i].astype(F32)
    out[0, :, pl.ds(pl.multiple_of(step * HD, HD), HD)] = summed[:, :HD]
    out[0, :, pl.ds(pl.multiple_of((KV_HEADS + step) * HD, HD), HD)] = summed[:, HD:]


def add_terms(terms):
    return pl.pallas_call(
        add_terms_kernel,
        grid=(KV_HEADS,),
        in_specs=[pl.BlockSpec((4, OWN, 2 * HD), lambda i: (i, 0, 0))],
        out_specs=full((1, OWN, 2 * KV_HEADS * HD)),
        out_shape=jax.ShapeDtypeStruct((1, OWN, 2 * KV_HEADS * HD), F32),
        compiler_params=params(),
        name="add_terms",
    )(terms)


def exchange(array, axes):
    return lax.all_to_all(array, axes, split_axis=0, concat_axis=0, tiled=True)


def per_device(roll_query, roll_keyval, roll_grad, prompt_keyval, lengths, send_rows, land_rows):
    where_x = lax.axis_index("x").astype(jnp.int32).reshape(1)
    prompt = pack_prompt(prompt_keyval[0], land_rows, lengths)
    prompt = exchange(prompt.reshape(-1, OWN + META, 2 * HD), ("yl", "z", "x"))
    received = []
    start = 0
    for heads in CHUNKS:
        rows = pack_rows(heads, start, start == 0, roll_query, roll_grad, roll_keyval, send_rows)
        rows = exchange(rows.reshape(32, 32, -1), ("grp", "yl", "z"))
        received.append(rows.reshape(4, KV_HEADS, 32, -1))
        start += heads
    far = near = None
    returned = []
    for index, heads in enumerate(CHUNKS):
        last = index == len(CHUNKS) - 1
        results = attend(
            heads, index == 0, last, where_x, prompt, received[index], received[0], CHUNKS[0], far, near
        )
        returned.append(exchange(results[0], ("yl", "z")))
        far = results[1]
        near = None if last else results[2]
    prompt_grad = add_terms(exchange(far, ("yl", "z", "x")))
    attn_out, query_grad, pair_grad = unpack(CHUNKS, returned)
    return attn_out, query_grad, pair_grad, prompt_grad


def solution(mesh):
    mesh = Mesh(mesh.devices.reshape(4, 2, 4, 4), ("grp", "yl", "z", "x"))
    rows = P(("grp", "yl", "z", "x"), None)
    placed = P("grp", ("yl", "z", "x"), None)
    return jax.shard_map(
        per_device,
        mesh=mesh,
        in_specs=(rows, rows, rows, placed, P("grp", ("yl", "z", "x")), placed, placed),
        out_specs=(rows, rows, rows, placed),
        check_vma=False,
    )
```

```python
import functools
import math

import jax
import jax.numpy as jnp
from jax import lax
from jax.experimental import pallas as pl
from jax.experimental.pallas import tpu as pltpu
from jax.sharding import Mesh, PartitionSpec as P

KV_HEADS = 8
GROUP = 8
HD = 128
ROWS = 128
RESP_LEN = 64
NPOS = 2048
OWN = 64
META = 16
SCALE = 1.0 / math.sqrt(HD)
EXP_SCALE = SCALE * math.log2(math.e)
F32 = jnp.float32
BF = jnp.bfloat16
NN = ((1,), (0,))
NT = ((1,), (1,))

CHUNKS = (4, 4)
TILE_ROWS = 512
POS_BLOCK = 512
VMEM = 56 * 1024 * 1024


def dot(a, b, dims):
    return lax.dot_general(a, b, (dims, ((), ())), preferred_element_type=F32)


def full(shape):
    return pl.BlockSpec(shape, lambda i: (0,) * len(shape))


def params():
    return pltpu.CompilerParams(dimension_semantics=("arbitrary",), vmem_limit_bytes=VMEM)


def one_hot_rows(picks):
    chosen = lax.broadcasted_iota(jnp.int32, (ROWS, ROWS), 0) == picks
    return jnp.transpose(chosen.astype(F32)).astype(BF)


def partner(place, slot, sign):
    turn = (place[1] + sign * (slot % 4) + 4) % 4
    return ((place[0] + slot // 4) % 2) * 4 + turn


def pack_prompt_kernel(place, land, lens, *refs):
    blocks, outs = refs[:4], refs[4:]
    lane = lax.broadcasted_iota(jnp.int32, (META, HD), 1)
    counts = jnp.where(lane == 0, lens[:, 0:1], lens[:, 1:2]).astype(F32).astype(BF)
    rows = jnp.broadcast_to(land[0], (META, HD)).astype(F32).astype(BF)
    for slot, out in enumerate(outs):
        head = partner(place, slot, 1)
        key_at = pl.ds(pl.multiple_of(head * HD, HD), HD)
        value_at = pl.ds(pl.multiple_of((KV_HEADS + head) * HD, HD), HD)
        for i, block in enumerate(blocks):
            out[i * OWN : (i + 1) * OWN, :HD] = block[:, key_at]
            out[i * OWN : (i + 1) * OWN, HD:] = block[:, value_at]
        out[4 * OWN :, :HD] = rows
        out[4 * OWN :, HD:] = counts


def pack_prompt(place, land, lens, blocks):
    shape = (4 * OWN + META, 2 * HD)
    return pl.pallas_call(
        pack_prompt_kernel,
        grid=(1,),
        in_specs=[pl.BlockSpec(memory_space=pltpu.SMEM), full((1, 1, ROWS)), full((1, 2))]
        + [full((OWN, 2 * KV_HEADS * HD))] * 4,
        out_specs=[full(shape)] * KV_HEADS,
        out_shape=[jax.ShapeDtypeStruct(shape, BF)] * KV_HEADS,
        compiler_params=params(),
        name="pack_prompt",
    )(place, land, lens, *blocks)


def pack_rows_kernel(wide, per_step, send, *refs):
    out = refs[-1]
    order = one_hot_rows(send[0])
    for a in range(per_step):
        for ref, at in zip((refs[a], refs[per_step + a]), (0, wide)):
            moved = dot(order, ref[...], NN).astype(BF)
            out[:, a, :, at : at + wide] = moved.reshape(4, 32, wide)
        for ref, at in zip(refs[2 * per_step : -1], (2 * wide, 2 * wide + HD)):
            moved = dot(order, ref[:, a * HD : (a + 1) * HD], NN).astype(BF)
            out[:, a, :, at : at + HD] = moved.reshape(4, 32, HD)


def pack_rows(heads, start, with_pair, query, grad, pair, send):
    wide = heads * HD
    per = GROUP // heads
    first = start // heads
    per_step = 4
    steps = KV_HEADS // per_step
    specs = [full((1, 1, ROWS))]
    for _ in range(2):
        for a in range(per_step):
            specs.append(pl.BlockSpec((ROWS, wide), lambda i, a=a: (0, (i * per_step + a) * per + first)))
    arrays = [send] + [query] * per_step + [grad] * per_step
    width = 2 * wide
    if with_pair:
        specs += [
            pl.BlockSpec((ROWS, per_step * HD), lambda i: (0, i)),
            pl.BlockSpec((ROWS, per_step * HD), lambda i: (0, steps + i)),
        ]
        arrays += [pair, pair]
        width += 2 * HD
    return pl.pallas_call(
        functools.partial(pack_rows_kernel, wide, per_step),
        grid=(steps,),
        in_specs=specs,
        out_specs=pl.BlockSpec((4, per_step, 32, width), lambda i: (0, i, 0, 0)),
        out_shape=jax.ShapeDtypeStruct((4, KV_HEADS, 32, width), BF),
        compiler_params=params(),
        name="pack_rows",
    )(*arrays)


def attend_kernel(heads, first, last, tile, *refs):
    refs = list(refs)
    place, rows_ref = refs[:2]
    prompts = refs[2 : 2 + KV_HEADS]
    refs = refs[2 + KV_HEADS :]
    if not first:
        pair_ref, far_in, near_in = refs[:3]
        refs = refs[3:]
    out = refs[0]
    if last:
        far_own, far_sent = refs[1], refs[2:5]
        refs = refs[5:]
    else:
        far_out, near_out = refs[1:3]
        refs = refs[3:]
    key_far, value_far, metas, expo, rounded, key_sum, value_sum = refs
    step = pl.program_id(0)
    wide = heads * HD
    held = 4 * OWN

    @pl.when(step == 0)
    def _():
        for slot, prompt in enumerate(prompts):
            key_far[slot * held : (slot + 1) * held] = prompt[:held, :HD]
            value_far[slot * held : (slot + 1) * held] = prompt[:held, HD:]
            metas[slot] = prompt[held:, :]
        if first:
            key_sum[...] = jnp.zeros_like(key_sum)
            value_sum[...] = jnp.zeros_like(value_sum)
        else:
            key_sum[...] = far_in[0]
            value_sum[...] = far_in[1]

    source = ((place[0] + step // 4) % 2) * 4 + (place[1] + 4 - step % 4) % 4
    meta = metas[source].astype(F32)
    order = one_hot_rows(meta[0:1, :HD].astype(jnp.int32))
    moved = dot(order, rows_ref[:, 0].reshape(ROWS, -1), NN).astype(BF)
    if first:
        pair = moved[:, 2 * wide :]
    else:
        pair = dot(order, pair_ref[:, 0].reshape(ROWS, -1), NN).astype(BF)
    key_near = pair[:, :HD]
    value_near = pair[:, HD:]

    row = lax.broadcasted_iota(jnp.int32, (ROWS, 1), 0)
    count = jnp.where(row < RESP_LEN, meta[0:1, HD : HD + 1], meta[0:1, HD + 1 : HD + 2] + RESP_LEN)
    live = (row.astype(F32) < count).astype(F32)
    at = lax.broadcasted_iota(jnp.int32, (ROWS, ROWS), 0)
    of = lax.broadcasted_iota(jnp.int32, (ROWS, ROWS), 1)
    seen = (of <= at) & ((of // RESP_LEN) == (at // RESP_LEN))
    hide = jnp.where(seen, 0.0, -1e30).astype(F32)
    per = tile // ROWS
    live = jnp.concatenate([live] * per, 0)
    hide = jnp.concatenate([hide] * per, 0)
    key_own = jnp.zeros((HD, ROWS), F32)
    value_own = jnp.zeros((HD, ROWS), F32)
    blocks = [slice(b, b + POS_BLOCK) for b in range(0, NPOS, POS_BLOCK)]
    lanes = [slice(j, j + HD) for j in range(0, POS_BLOCK, HD)]
    for part in range(heads // per):
        cols = [slice((part * per + a) * HD, (part * per + a + 1) * HD) for a in range(per)]
        query = jnp.concatenate([moved[:, c] for c in cols], 0)
        grad = jnp.concatenate([moved[:, wide + c.start : wide + c.stop] for c in cols], 0)
        query_t = query.T
        grad_t = grad.T
        score_near = dot(query, key_near, NT) + hide
        largest = score_near
        for b in blocks:
            score = dot(query, key_far[b], NT)
            expo[:, b] = score
            for j in lanes:
                largest = jnp.maximum(largest, score[:, j])
        shift = jnp.max(largest, axis=1, keepdims=True) * EXP_SCALE
        exp_near = jnp.exp2(score_near * EXP_SCALE - shift)
        total = exp_near
        for b in blocks:
            value = jnp.exp2(expo[:, b] * EXP_SCALE - shift)
            expo[:, b] = value
            for j in lanes:
                total = total + value[:, j]
        factor = live / jnp.sum(total, axis=1, keepdims=True)
        rounded_near = (exp_near * factor).astype(BF)
        attended = dot(rounded_near, value_near, NN)
        for b in blocks:
            weight = (expo[:, b] * factor).astype(BF)
            rounded[:, b] = weight
            attended = attended + dot(weight, value_far[b], NN)
        attended = attended.astype(BF)
        delta = jnp.sum(grad.astype(F32) * attended.astype(F32), axis=1, keepdims=True)
        scaled = factor * SCALE
        slope = (exp_near * scaled * (dot(grad, value_near, NT) - delta)).astype(BF)
        query_grad = dot(slope, key_near, NN)
        key_own = key_own + dot(query_t, slope, NN)
        value_own = value_own + dot(grad_t, rounded_near, NN)
        for b in blocks:
            slope = (expo[:, b] * scaled * (dot(grad, value_far[b], NT) - delta)).astype(BF)
            query_grad = query_grad + dot(slope, key_far[b], NN)
            key_sum[:, b] += dot(query_t, slope, NN)
            value_sum[:, b] += dot(grad_t, rounded[:, b], NN)
        query_grad = query_grad.astype(BF)
        for a, c in enumerate(cols):
            own = slice(a * ROWS, (a + 1) * ROWS)
            out[0, :, c] = attended[own]
            out[0, :, wide + c.start : wide + c.stop] = query_grad[own]
    if not first:
        key_own = key_own + near_in[0, 0]
        value_own = value_own + near_in[0, 1]
    if last:
        out[0, :, 2 * wide : 2 * wide + HD] = key_own.T.astype(BF)
        out[0, :, 2 * wide + HD :] = value_own.T.astype(BF)
    else:
        near_out[0, 0] = key_own
        near_out[0, 1] = value_own

    @pl.when(step == KV_HEADS - 1)
    def _():
        if last:
            for half, summed in ((slice(0, HD), key_sum), (slice(HD, 2 * HD), value_sum)):
                terms = summed[...].T.reshape(KV_HEADS, 4, OWN, HD)
                far_own[:, :, half] = terms[:, 0]
                for i in range(3):
                    far_sent[i][:, :, half] = terms[:, i + 1].astype(BF)
        else:
            far_out[0] = key_sum[...]
            far_out[1] = value_sum[...]


def attend(heads, first, last, place, prompts, rows, pair_rows, pair_lane, far, near):
    tile = min(TILE_ROWS, heads * ROWS)
    wide = 2 * heads * HD
    width_in = wide + (2 * HD if first else 0)
    width_out = wide + (2 * HD if last else 0)
    near_spec = pl.BlockSpec((1, 2, HD, ROWS), lambda i: (i, 0, 0, 0))
    arrays = [place, rows, *prompts]
    specs = [
        pl.BlockSpec(memory_space=pltpu.SMEM),
        pl.BlockSpec((4, 1, 32, width_in), lambda i: (0, i, 0, 0)),
    ]
    specs += [full((4 * OWN + META, 2 * HD))] * KV_HEADS
    if not first:
        arrays += [pair_rows, far, near]
        specs += [
            pl.BlockSpec((4, 1, 32, 2 * HD), lambda i: (0, i, 0, pair_lane)),
            full((2, HD, NPOS)),
            near_spec,
        ]
    shapes = [jax.ShapeDtypeStruct((KV_HEADS, ROWS, width_out), BF)]
    out_specs = [pl.BlockSpec((1, ROWS, width_out), lambda i: (i, 0, 0))]
    if last:
        term = (KV_HEADS, OWN, 2 * HD)
        shapes += [jax.ShapeDtypeStruct(term, F32)] + [jax.ShapeDtypeStruct(term, BF)] * 3
        out_specs += [full(term)] * 4
    else:
        shapes.append(jax.ShapeDtypeStruct((2, HD, NPOS), F32))
        out_specs.append(full((2, HD, NPOS)))
        shapes.append(jax.ShapeDtypeStruct((KV_HEADS, 2, HD, ROWS), F32))
        out_specs.append(near_spec)
    return pl.pallas_call(
        functools.partial(attend_kernel, heads, first, last, tile),
        grid=(KV_HEADS,),
        in_specs=specs,
        out_specs=out_specs,
        out_shape=shapes,
        scratch_shapes=[
            pltpu.VMEM((NPOS, HD), BF),
            pltpu.VMEM((NPOS, HD), BF),
            pltpu.VMEM((KV_HEADS, META, 2 * HD), BF),
            pltpu.VMEM((tile, NPOS), F32),
            pltpu.VMEM((tile, NPOS), BF),
            pltpu.VMEM((HD, NPOS), F32),
            pltpu.VMEM((HD, NPOS), F32),
        ],
        compiler_params=params(),
        name="attend",
    )(*arrays)


def unpack_kernel(heads, with_pair, ref, *refs):
    outs = refs[-3:] if with_pair else refs[-2:]
    step = pl.program_id(0)
    wide = heads * HD
    outs[0][...] = ref[0, :, :wide]
    outs[1][...] = ref[0, :, wide : 2 * wide]
    if with_pair:
        key_at = pl.ds(pl.multiple_of(step * HD, HD), HD)
        value_at = pl.ds(pl.multiple_of((KV_HEADS + step) * HD, HD), HD)
        outs[2][:, key_at] = ref[0, :, 2 * wide : 2 * wide + HD]
        outs[2][:, value_at] = ref[0, :, 2 * wide + HD :]


def unpack(heads, start, with_pair, array, filled):
    wide = heads * HD
    per = GROUP // heads
    first = start // heads
    spec = pl.BlockSpec((ROWS, wide), lambda i: (0, i * per + first))
    shapes = [jax.ShapeDtypeStruct((ROWS, KV_HEADS * GROUP * HD), BF)] * 2
    out_specs = [spec, spec]
    if with_pair:
        shapes.append(jax.ShapeDtypeStruct((ROWS, 2 * KV_HEADS * HD), BF))
        out_specs.append(full((ROWS, 2 * KV_HEADS * HD)))
    return pl.pallas_call(
        functools.partial(unpack_kernel, heads, with_pair),
        grid=(KV_HEADS,),
        in_specs=[pl.BlockSpec((1,) + array.shape[1:], lambda i: (i, 0, 0))]
        + [pl.BlockSpec(memory_space=pl.ANY)] * len(filled),
        out_specs=out_specs,
        out_shape=shapes,
        input_output_aliases={1 + i: i for i in range(len(filled))},
        compiler_params=params(),
        name="unpack",
    )(array, *filled)


def add_terms_kernel(own, *refs):
    terms, outs = refs[:3], refs[3:]
    for slot, out in enumerate(outs):
        summed = own[slot]
        for term in terms:
            summed = summed + term[slot].astype(F32)
        out[...] = summed


def add_terms(own, terms):
    shape = (KV_HEADS, OWN, 2 * HD)
    return pl.pallas_call(
        add_terms_kernel,
        grid=(1,),
        in_specs=[full(shape)] * 4,
        out_specs=[full(shape[1:])] * KV_HEADS,
        out_shape=[jax.ShapeDtypeStruct(shape[1:], F32)] * KV_HEADS,
        compiler_params=params(),
        name="add_terms",
    )(own, *terms)


def place_terms_kernel(place, *refs):
    out = refs[-1]
    for slot, term in enumerate(refs[:-1]):
        head = partner(place, slot, 1)
        out[0, :, pl.ds(pl.multiple_of(head * HD, HD), HD)] = term[:, :HD]
        out[0, :, pl.ds(pl.multiple_of((KV_HEADS + head) * HD, HD), HD)] = term[:, HD:]


def place_terms(place, terms):
    shape = (1, OWN, 2 * KV_HEADS * HD)
    return pl.pallas_call(
        place_terms_kernel,
        grid=(1,),
        in_specs=[pl.BlockSpec(memory_space=pltpu.SMEM)] + [full((OWN, 2 * HD))] * KV_HEADS,
        out_specs=full(shape),
        out_shape=jax.ShapeDtypeStruct(shape, F32),
        compiler_params=params(),
        name="place_terms",
    )(place, *terms)


def exchange(array, axes):
    return lax.all_to_all(array, axes, split_axis=0, concat_axis=0, tiled=True)


def shift_x(array, by):
    return lax.ppermute(array, "x", [(i, (i + by) % 4) for i in range(4)])


def shift_head(array, slot, sign):
    pairs = []
    for yl in range(2):
        for z in range(4):
            there = ((yl + slot // 4) % 2) * 4 + (z + sign * (slot % 4)) % 4
            pairs.append((yl * 4 + z, there))
    return lax.ppermute(array, ("yl", "z"), pairs)


def per_device(roll_query, roll_keyval, roll_grad, prompt_keyval, lengths, send_rows, land_rows):
    place = jnp.stack([lax.axis_index("yl"), lax.axis_index("z")]).astype(jnp.int32)
    own = prompt_keyval[0]
    blocks = [own] + [shift_x(own, i) for i in range(1, 4)]
    prompts = pack_prompt(place, land_rows, lengths, blocks)
    prompts = [prompts[0]] + [shift_head(prompts[k], k, 1) for k in range(1, KV_HEADS)]
    received = []
    start = 0
    for heads in CHUNKS:
        rows = pack_rows(heads, start, start == 0, roll_query, roll_grad, roll_keyval, send_rows)
        if len(received) == 1:
            rows, prompts, received = lax.optimization_barrier((rows, prompts, received))
        rows = exchange(rows.reshape(32, 32, -1), ("grp", "yl", "z"))
        received.append(rows.reshape(4, KV_HEADS, 32, -1))
        start += heads
    returned = []
    carried = (None, None)
    for index, heads in enumerate(CHUNKS):
        last = index == len(CHUNKS) - 1
        results = attend(
            heads, index == 0, last, place, prompts, received[index], received[0], CHUNKS[0], *carried
        )
        carried = results[1:]
        if returned:
            results, earlier = lax.optimization_barrier((results, returned[-1]))
            returned[-1] = earlier
            carried = results[1:]
        returned.append(exchange(results[0], ("yl", "z")))
    terms = add_terms(carried[0], [shift_x(carried[i], -i) for i in range(1, 4)])
    terms = [terms[0]] + [shift_head(terms[k], k, -1) for k in range(1, KV_HEADS)]
    prompt_grad = place_terms(place, terms)
    filled = ()
    start = 0
    for index, heads in enumerate(CHUNKS):
        filled = unpack(heads, start, index == len(CHUNKS) - 1, returned[index], filled[:2])
        start += heads
    return (*filled, prompt_grad)


def solution(mesh):
    mesh = Mesh(mesh.devices.reshape(4, 2, 4, 4), ("grp", "yl", "z", "x"))
    rows = P(("grp", "yl", "z", "x"), None)
    placed = P("grp", ("yl", "z", "x"), None)
    return jax.shard_map(
        per_device,
        mesh=mesh,
        in_specs=(rows, rows, rows, placed, P("grp", ("yl", "z", "x")), placed, placed),
        out_specs=(rows, rows, rows, placed),
        check_vma=False,
    )
```

```python
import functools
import math

import jax
import jax.numpy as jnp
from jax import lax
from jax.experimental import pallas as pl
from jax.experimental.pallas import tpu as pltpu
from jax.sharding import Mesh, PartitionSpec as P

KV_HEADS = 8
GROUP = 8
HD = 128
ROWS = 128
RESP_LEN = 64
NPOS = 2048
OWN = 64
META = 16
SCALE = 1.0 / math.sqrt(HD)
EXP_SCALE = SCALE * math.log2(math.e)
F32 = jnp.float32
BF = jnp.bfloat16
NN = ((1,), (0,))
NT = ((1,), (1,))

CHUNKS = (4, 4)
TILE_ROWS = 512
POS_BLOCK = 512
PER_STEP = 4
VMEM = 60 * 1024 * 1024


def dot(a, b, dims):
    return lax.dot_general(a, b, (dims, ((), ())), preferred_element_type=F32)


def full(shape):
    return pl.BlockSpec(shape, lambda i: (0,) * len(shape))


def params():
    return pltpu.CompilerParams(dimension_semantics=("arbitrary",), vmem_limit_bytes=VMEM)


def one_hot_rows(picks):
    chosen = lax.broadcasted_iota(jnp.int32, (ROWS, ROWS), 0) == picks
    return jnp.transpose(chosen.astype(F32)).astype(BF)


def pack_prompt_kernel(prompt, land, lens, out):
    lane = lax.broadcasted_iota(jnp.int32, (META, HD), 1)
    counts = jnp.where(lane == 0, lens[:, 0:1], lens[:, 1:2]).astype(F32).astype(BF)
    rows = jnp.broadcast_to(land[0], (META, HD)).astype(F32).astype(BF)
    for head in range(KV_HEADS):
        value_at = (KV_HEADS + head) * HD
        out[head, :OWN, :HD] = prompt[:, head * HD : (head + 1) * HD]
        out[head, :OWN, HD:] = prompt[:, value_at : value_at + HD]
        out[head, OWN:, :HD] = rows
        out[head, OWN:, HD:] = counts


def pack_prompt(prompt, land, lens):
    shape = (KV_HEADS, OWN + META, 2 * HD)
    return pl.pallas_call(
        pack_prompt_kernel,
        grid=(1,),
        in_specs=[full((OWN, 2 * KV_HEADS * HD)), full((1, 1, ROWS)), full((1, 2))],
        out_specs=full(shape),
        out_shape=jax.ShapeDtypeStruct(shape, BF),
        compiler_params=params(),
        name="pack_prompt",
    )(prompt, land, lens)


def pack_rows_kernel(wide, per_step, send, *refs):
    out = refs[-1]
    order = one_hot_rows(send[0])
    for a in range(per_step):
        for ref, at in zip((refs[a], refs[per_step + a]), (0, wide)):
            moved = dot(order, ref[...], NN).astype(BF)
            out[:, a, :, at : at + wide] = moved.reshape(4, 32, wide)
        for ref, at in zip(refs[2 * per_step : -1], (2 * wide, 2 * wide + HD)):
            moved = dot(order, ref[:, a * HD : (a + 1) * HD], NN).astype(BF)
            out[:, a, :, at : at + HD] = moved.reshape(4, 32, HD)


def pack_rows(heads, start, with_pair, query, grad, pair, send):
    wide = heads * HD
    per = GROUP // heads
    first = start // heads
    per_step = 4
    steps = KV_HEADS // per_step
    specs = [full((1, 1, ROWS))]
    for _ in range(2):
        for a in range(per_step):
            specs.append(pl.BlockSpec((ROWS, wide), lambda i, a=a: (0, (i * per_step + a) * per + first)))
    arrays = [send] + [query] * per_step + [grad] * per_step
    width = 2 * wide
    if with_pair:
        specs += [
            pl.BlockSpec((ROWS, per_step * HD), lambda i: (0, i)),
            pl.BlockSpec((ROWS, per_step * HD), lambda i: (0, steps + i)),
        ]
        arrays += [pair, pair]
        width += 2 * HD
    return pl.pallas_call(
        functools.partial(pack_rows_kernel, wide, per_step),
        grid=(steps,),
        in_specs=specs,
        out_specs=pl.BlockSpec((4, per_step, 32, width), lambda i: (0, i, 0, 0)),
        out_shape=jax.ShapeDtypeStruct((4, KV_HEADS, 32, width), BF),
        compiler_params=params(),
        name="pack_rows",
    )(*arrays)


def attend_kernel(heads, first, last, tile, *refs):
    refs = list(refs)
    rows_ref, prompts = refs[0], refs[1:5]
    refs = refs[5:]
    if not first:
        pair_ref, far_in, near_in = refs[:3]
        refs = refs[3:]
    out = refs[0]
    if last:
        far_own, far_sent = refs[1], refs[2:5]
        refs = refs[5:]
    else:
        far_out, near_out = refs[1:3]
        refs = refs[3:]
    key_far, value_far, expo_even, expo_odd, rounded_even, rounded_odd, key_sum, value_sum = refs
    step = pl.program_id(0)
    wide = heads * HD
    held = KV_HEADS * OWN
    per = tile // ROWS
    parts = heads // per
    blocks = [slice(b, b + POS_BLOCK) for b in range(0, NPOS, POS_BLOCK)]
    lanes = [slice(j, j + HD) for j in range(0, POS_BLOCK, HD)]

    @pl.when(step == 0)
    def _():
        for i, prompt in enumerate(prompts):
            key_far[i * held : (i + 1) * held] = prompt[:, :OWN, :HD].reshape(held, HD)
            value_far[i * held : (i + 1) * held] = prompt[:, :OWN, HD:].reshape(held, HD)
        if first:
            key_sum[...] = jnp.zeros_like(key_sum)
            value_sum[...] = jnp.zeros_like(value_sum)
        else:
            key_sum[...] = far_in[0]
            value_sum[...] = far_in[1]

    row = lax.broadcasted_iota(jnp.int32, (ROWS, 1), 0)
    at = lax.broadcasted_iota(jnp.int32, (ROWS, ROWS), 0)
    of = lax.broadcasted_iota(jnp.int32, (ROWS, ROWS), 1)
    seen = (of <= at) & ((of // RESP_LEN) == (at // RESP_LEN))
    hide = jnp.concatenate([jnp.where(seen, 0.0, -1e30).astype(F32)] * per, 0)

    class Tile:
        pass

    tiles = []
    for source in range(PER_STEP):
        meta = prompts[0][step * PER_STEP + source, OWN:, :].astype(F32)
        order = one_hot_rows(meta[0:1, :HD].astype(jnp.int32))
        moved = dot(order, rows_ref[:, source].reshape(ROWS, -1), NN).astype(BF)
        if first:
            pair = moved[:, 2 * wide :]
        else:
            pair = dot(order, pair_ref[:, source].reshape(ROWS, -1), NN).astype(BF)
        count = jnp.where(
            row < RESP_LEN, meta[0:1, HD : HD + 1], meta[0:1, HD + 1 : HD + 2] + RESP_LEN
        )
        live = jnp.concatenate([(row.astype(F32) < count).astype(F32)] * per, 0)
        near = Tile()
        near.key, near.value = pair[:, :HD], pair[:, HD:]
        near.key_sum = jnp.zeros((HD, ROWS), F32) if first else near_in[source, 0]
        near.value_sum = jnp.zeros((HD, ROWS), F32) if first else near_in[source, 1]
        for part in range(parts):
            t = Tile()
            t.source, t.near, t.live, t.closes = source, near, live, part == parts - 1
            t.cols = [slice((part * per + a) * HD, (part * per + a + 1) * HD) for a in range(per)]
            t.query = jnp.concatenate([moved[:, c] for c in t.cols], 0)
            t.grad = jnp.concatenate([moved[:, wide + c.start : wide + c.stop] for c in t.cols], 0)
            odd = len(tiles) % 2
            t.expo, t.rounded = (expo_odd, rounded_odd) if odd else (expo_even, rounded_even)
            tiles.append(t)

    def score_near(t):
        t.score_near = dot(t.query, t.near.key, NT) + hide
        t.largest = t.score_near

    def score_far(t, b):
        score = dot(t.query, key_far[b], NT)
        t.expo[:, b] = score
        for j in lanes:
            t.largest = jnp.maximum(t.largest, score[:, j])

    def expo_near(t):
        t.shift = jnp.max(t.largest, axis=1, keepdims=True) * EXP_SCALE
        t.expo_near = jnp.exp2(t.score_near * EXP_SCALE - t.shift)
        t.total = t.expo_near

    def expo_far(t, b):
        value = jnp.exp2(t.expo[:, b] * EXP_SCALE - t.shift)
        t.expo[:, b] = value
        for j in lanes:
            t.total = t.total + value[:, j]

    def attend_near(t):
        t.factor = t.live / jnp.sum(t.total, axis=1, keepdims=True)
        t.rounded_near = (t.expo_near * t.factor).astype(BF)
        t.attended = dot(t.rounded_near, t.near.value, NN)

    def attend_far(t, b):
        weight = (t.expo[:, b] * t.factor).astype(BF)
        t.rounded[:, b] = weight
        t.attended = t.attended + dot(weight, value_far[b], NN)

    def slope_near(t):
        t.attended = t.attended.astype(BF)
        t.delta = jnp.sum(t.grad.astype(F32) * t.attended.astype(F32), axis=1, keepdims=True)
        t.scaled = t.factor * SCALE
        slope = t.expo_near * t.scaled * (dot(t.grad, t.near.value, NT) - t.delta)
        slope = slope.astype(BF)
        t.query_grad = dot(slope, t.near.key, NN)
        t.query_t, t.grad_t = t.query.T, t.grad.T
        t.near.key_sum = t.near.key_sum + dot(t.query_t, slope, NN)
        t.near.value_sum = t.near.value_sum + dot(t.grad_t, t.rounded_near, NN)

    def slope_far(t, b):
        slope = t.expo[:, b] * t.scaled * (dot(t.grad, value_far[b], NT) - t.delta)
        slope = slope.astype(BF)
        t.query_grad = t.query_grad + dot(slope, key_far[b], NN)
        key_sum[:, b] += dot(t.query_t, slope, NN)
        value_sum[:, b] += dot(t.grad_t, t.rounded[:, b], NN)

    def store(t):
        query_grad = t.query_grad.astype(BF)
        for a, c in enumerate(t.cols):
            own = slice(a * ROWS, (a + 1) * ROWS)
            out[t.source, :, c] = t.attended[own]
            out[t.source, :, wide + c.start : wide + c.stop] = query_grad[own]
        if t.closes and last:
            out[t.source, :, 2 * wide : 2 * wide + HD] = t.near.key_sum.T.astype(BF)
            out[t.source, :, 2 * wide + HD :] = t.near.value_sum.T.astype(BF)
        elif t.closes:
            near_out[t.source, 0] = t.near.key_sum
            near_out[t.source, 1] = t.near.value_sum

    score_near(tiles[0])
    for b in blocks:
        score_far(tiles[0], b)
    expo_near(tiles[0])
    for b in blocks:
        expo_far(tiles[0], b)
    for t, after in zip(tiles, tiles[1:] + [None]):
        attend_near(t)
        if after:
            score_near(after)
        for b in blocks:
            attend_far(t, b)
            if after:
                score_far(after, b)
        slope_near(t)
        if after:
            expo_near(after)
        for b in blocks:
            slope_far(t, b)
            if after:
                expo_far(after, b)
        store(t)

    @pl.when(step == KV_HEADS // PER_STEP - 1)
    def _():
        if last:
            for half, summed in ((slice(0, HD), key_sum), (slice(HD, 2 * HD), value_sum)):
                terms = summed[...].T.reshape(4, KV_HEADS, OWN, HD)
                far_own[:, :, half] = terms[0]
                for i in range(3):
                    far_sent[i][:, :, half] = terms[i + 1].astype(BF)
        else:
            far_out[0] = key_sum[...]
            far_out[1] = value_sum[...]


def attend(heads, first, last, prompts, rows, pair_rows, pair_lane, far, near):
    tile = min(TILE_ROWS, heads * ROWS)
    wide = 2 * heads * HD
    width_in = wide + (2 * HD if first else 0)
    width_out = wide + (2 * HD if last else 0)
    near_spec = pl.BlockSpec((PER_STEP, 2, HD, ROWS), lambda i: (i, 0, 0, 0))
    arrays = [rows, *prompts]
    specs = [pl.BlockSpec((4, PER_STEP, 32, width_in), lambda i: (0, i, 0, 0))]
    specs += [full((KV_HEADS, OWN + META, 2 * HD))] * 4
    if not first:
        arrays += [pair_rows, far, near]
        specs += [
            pl.BlockSpec((4, PER_STEP, 32, 2 * HD), lambda i: (0, i, 0, pair_lane)),
            full((2, HD, NPOS)),
            near_spec,
        ]
    shapes = [jax.ShapeDtypeStruct((KV_HEADS, ROWS, width_out), BF)]
    out_specs = [pl.BlockSpec((PER_STEP, ROWS, width_out), lambda i: (i, 0, 0))]
    if last:
        term = (KV_HEADS, OWN, 2 * HD)
        shapes += [jax.ShapeDtypeStruct(term, F32)] + [jax.ShapeDtypeStruct(term, BF)] * 3
        out_specs += [full(term)] * 4
    else:
        shapes.append(jax.ShapeDtypeStruct((2, HD, NPOS), F32))
        out_specs.append(full((2, HD, NPOS)))
        shapes.append(jax.ShapeDtypeStruct((KV_HEADS, 2, HD, ROWS), F32))
        out_specs.append(near_spec)
    return pl.pallas_call(
        functools.partial(attend_kernel, heads, first, last, tile),
        grid=(KV_HEADS // PER_STEP,),
        in_specs=specs,
        out_specs=out_specs,
        out_shape=shapes,
        scratch_shapes=[
            pltpu.VMEM((NPOS, HD), BF),
            pltpu.VMEM((NPOS, HD), BF),
            pltpu.VMEM((tile, NPOS), F32),
            pltpu.VMEM((tile, NPOS), F32),
            pltpu.VMEM((tile, NPOS), BF),
            pltpu.VMEM((tile, NPOS), BF),
            pltpu.VMEM((HD, NPOS), F32),
            pltpu.VMEM((HD, NPOS), F32),
        ],
        compiler_params=params(),
        name="attend",
    )(*arrays)


def unpack_kernel(heads, start, with_pair, filled, ref, *refs):
    outs, done = refs[filled:-1], refs[-1]
    wide = heads * HD
    moves = []
    for head in range(KV_HEADS):
        at = pl.ds((head * GROUP + start) * HD, wide)
        moves.append((ref.at[head, :, pl.ds(0, wide)], outs[0].at[:, at]))
        moves.append((ref.at[head, :, pl.ds(wide, wide)], outs[1].at[:, at]))
        if with_pair:
            for half in range(2):
                part = ref.at[head, :, pl.ds(2 * wide + half * HD, HD)]
                moves.append((part, outs[2].at[:, pl.ds((half * KV_HEADS + head) * HD, HD)]))
    copies = [pltpu.make_async_copy(a, b, done.at[i]) for i, (a, b) in enumerate(moves)]
    for copy in copies:
        copy.start()
    for copy in copies:
        copy.wait()


def unpack(heads, start, with_pair, array, filled):
    shapes = [jax.ShapeDtypeStruct((ROWS, KV_HEADS * GROUP * HD), BF)] * 2
    if with_pair:
        shapes.append(jax.ShapeDtypeStruct((ROWS, 2 * KV_HEADS * HD), BF))
    return pl.pallas_call(
        functools.partial(unpack_kernel, heads, start, with_pair, len(filled)),
        in_specs=[pl.BlockSpec(memory_space=pl.ANY)] * (1 + len(filled)),
        out_specs=[pl.BlockSpec(memory_space=pl.ANY)] * len(shapes),
        out_shape=shapes,
        scratch_shapes=[pltpu.SemaphoreType.DMA((4 * KV_HEADS,))],
        input_output_aliases={1 + i: i for i in range(len(filled))},
        compiler_params=pltpu.CompilerParams(vmem_limit_bytes=VMEM),
        name="unpack",
    )(array, *filled)


def add_terms_kernel(own, *refs):
    out = refs[-1]
    summed = own[...]
    for term in refs[:-1]:
        summed = summed + term[...].astype(F32)
    out[...] = summed


def add_terms(own, terms):
    shape = (KV_HEADS, OWN, 2 * HD)
    return pl.pallas_call(
        add_terms_kernel,
        grid=(1,),
        in_specs=[full(shape)] * 4,
        out_specs=full(shape),
        out_shape=jax.ShapeDtypeStruct(shape, F32),
        compiler_params=params(),
        name="add_terms",
    )(own, *terms)


def place_terms_kernel(terms, out):
    for head in range(KV_HEADS):
        value_at = (KV_HEADS + head) * HD
        out[0, :, head * HD : (head + 1) * HD] = terms[head, :, :HD]
        out[0, :, value_at : value_at + HD] = terms[head, :, HD:]


def place_terms(terms):
    shape = (1, OWN, 2 * KV_HEADS * HD)
    return pl.pallas_call(
        place_terms_kernel,
        grid=(1,),
        in_specs=[full((KV_HEADS, OWN, 2 * HD))],
        out_specs=full(shape),
        out_shape=jax.ShapeDtypeStruct(shape, F32),
        compiler_params=params(),
        name="place_terms",
    )(terms)


def exchange(array, axes):
    return lax.all_to_all(array, axes, split_axis=0, concat_axis=0, tiled=True)


def shift_x(array, by):
    return lax.ppermute(array, "x", [(i, (i + by) % 4) for i in range(4)])


def per_device(roll_query, roll_keyval, roll_grad, prompt_keyval, lengths, send_rows, land_rows):
    prompt = exchange(pack_prompt(prompt_keyval[0], land_rows, lengths), ("yl", "z"))
    rows = []
    start = 0
    for heads in CHUNKS:
        rows.append(pack_rows(heads, start, start == 0, roll_query, roll_grad, roll_keyval, send_rows))
        start += heads
    rows[0], prompt = lax.optimization_barrier((rows[0], prompt))
    prompts = [prompt] + [shift_x(prompt, i) for i in range(1, 4)]
    received = []
    for packed in rows:
        if len(received) == 1:
            packed, prompts, received = lax.optimization_barrier((packed, prompts, received))
        packed = exchange(packed.reshape(32, 32, -1), ("grp", "yl", "z"))
        received.append(packed.reshape(4, KV_HEADS, 32, -1))
    returned = []
    carried = (None, None)
    for index, heads in enumerate(CHUNKS):
        last = index == len(CHUNKS) - 1
        results = attend(
            heads, index == 0, last, prompts, received[index], received[0], CHUNKS[0], *carried
        )
        carried = results[1:]
        if returned:
            results, earlier = lax.optimization_barrier((results, returned[-1]))
            returned[-1] = earlier
            carried = results[1:]
        returned.append(exchange(results[0], ("yl", "z")))
    terms = add_terms(carried[0], [shift_x(carried[i], -i) for i in range(1, 4)])
    terms, returned[-1] = lax.optimization_barrier((terms, returned[-1]))
    prompt_grad = place_terms(exchange(terms, ("yl", "z")))
    filled = ()
    start = 0
    for index, heads in enumerate(CHUNKS):
        filled = unpack(heads, start, index == len(CHUNKS) - 1, returned[index], filled[:2])
        start += heads
    return (*filled, prompt_grad)


def solution(mesh):
    mesh = Mesh(mesh.devices.reshape(4, 2, 4, 4), ("grp", "yl", "z", "x"))
    rows = P(("grp", "yl", "z", "x"), None)
    placed = P("grp", ("yl", "z", "x"), None)
    return jax.shard_map(
        per_device,
        mesh=mesh,
        in_specs=(rows, rows, rows, placed, P("grp", ("yl", "z", "x")), placed, placed),
        out_specs=(rows, rows, rows, placed),
        check_vma=False,
    )
```

```python
import functools
import math

import jax
import jax.numpy as jnp
from jax import lax
from jax.experimental import pallas as pl
from jax.experimental.pallas import tpu as pltpu
from jax.sharding import Mesh, PartitionSpec as P

KV_HEADS = 8
GROUP = 8
HD = 128
ROWS = 128
RESP_LEN = 64
NPOS = 2048
OWN = 64
META = 16
SCALE = 1.0 / math.sqrt(HD)
EXP_SCALE = SCALE * math.log2(math.e)
F32 = jnp.float32
BF = jnp.bfloat16
NN = ((1,), (0,))
NT = ((1,), (1,))

CHUNKS = (4, 4)
TILE_ROWS = 512
POS_BLOCK = 1024
PER_STEP = 4
VMEM = 60 * 1024 * 1024


def dot(a, b, dims):
    return lax.dot_general(a, b, (dims, ((), ())), preferred_element_type=F32)


def full(shape):
    return pl.BlockSpec(shape, lambda i: (0,) * len(shape))


def params():
    return pltpu.CompilerParams(dimension_semantics=("arbitrary",), vmem_limit_bytes=VMEM)


def one_hot_rows(picks):
    chosen = lax.broadcasted_iota(jnp.int32, (ROWS, ROWS), 0) == picks
    return jnp.transpose(chosen.astype(F32)).astype(BF)


def pack_prompt_kernel(prompt, land, lens, out):
    lane = lax.broadcasted_iota(jnp.int32, (META, HD), 1)
    counts = jnp.where(lane == 0, lens[:, 0:1], lens[:, 1:2]).astype(F32).astype(BF)
    rows = jnp.broadcast_to(land[0], (META, HD)).astype(F32).astype(BF)
    for head in range(KV_HEADS):
        value_at = (KV_HEADS + head) * HD
        out[head, :OWN, :HD] = prompt[:, head * HD : (head + 1) * HD]
        out[head, :OWN, HD:] = prompt[:, value_at : value_at + HD]
        out[head, OWN:, :HD] = rows
        out[head, OWN:, HD:] = counts


def pack_prompt(prompt, land, lens):
    shape = (KV_HEADS, OWN + META, 2 * HD)
    return pl.pallas_call(
        pack_prompt_kernel,
        grid=(1,),
        in_specs=[full((OWN, 2 * KV_HEADS * HD)), full((1, 1, ROWS)), full((1, 2))],
        out_specs=full(shape),
        out_shape=jax.ShapeDtypeStruct(shape, BF),
        compiler_params=params(),
        name="pack_prompt",
    )(prompt, land, lens)


def pack_rows_kernel(wide, per_step, send, *refs):
    out = refs[-1]
    order = one_hot_rows(send[0])
    for a in range(per_step):
        for ref, at in zip((refs[a], refs[per_step + a]), (0, wide)):
            moved = dot(order, ref[...], NN).astype(BF)
            out[:, a, :, at : at + wide] = moved.reshape(4, 32, wide)
        for ref, at in zip(refs[2 * per_step : -1], (2 * wide, 2 * wide + HD)):
            moved = dot(order, ref[:, a * HD : (a + 1) * HD], NN).astype(BF)
            out[:, a, :, at : at + HD] = moved.reshape(4, 32, HD)


def pack_rows(heads, start, with_pair, query, grad, pair, send):
    wide = heads * HD
    per = GROUP // heads
    first = start // heads
    per_step = 4
    steps = KV_HEADS // per_step
    specs = [full((1, 1, ROWS))]
    for _ in range(2):
        for a in range(per_step):
            specs.append(pl.BlockSpec((ROWS, wide), lambda i, a=a: (0, (i * per_step + a) * per + first)))
    arrays = [send] + [query] * per_step + [grad] * per_step
    width = 2 * wide
    if with_pair:
        specs += [
            pl.BlockSpec((ROWS, per_step * HD), lambda i: (0, i)),
            pl.BlockSpec((ROWS, per_step * HD), lambda i: (0, steps + i)),
        ]
        arrays += [pair, pair]
        width += 2 * HD
    return pl.pallas_call(
        functools.partial(pack_rows_kernel, wide, per_step),
        grid=(steps,),
        in_specs=specs,
        out_specs=pl.BlockSpec((4, per_step, 32, width), lambda i: (0, i, 0, 0)),
        out_shape=jax.ShapeDtypeStruct((4, KV_HEADS, 32, width), BF),
        compiler_params=params(),
        name="pack_rows",
    )(*arrays)


def attend_kernel(heads, first, last, tile, *refs):
    refs = list(refs)
    rows_ref, prompts = refs[0], refs[1:5]
    refs = refs[5:]
    if not first:
        pair_ref, far_in, near_in = refs[:3]
        refs = refs[3:]
    out = refs[0]
    if last:
        far_own, far_sent = refs[1], refs[2:5]
        refs = refs[5:]
    else:
        far_out, near_out = refs[1:3]
        refs = refs[3:]
    key_far, value_far, expo_even, expo_odd, rounded_even, rounded_odd, key_sum, value_sum = refs
    step = pl.program_id(0)
    wide = heads * HD
    held = KV_HEADS * OWN
    per = tile // ROWS
    parts = heads // per
    blocks = [slice(b, b + POS_BLOCK) for b in range(0, NPOS, POS_BLOCK)]
    lanes = [slice(j, j + HD) for j in range(0, POS_BLOCK, HD)]

    @pl.when(step == 0)
    def _():
        for i, prompt in enumerate(prompts):
            key_far[i * held : (i + 1) * held] = prompt[:, :OWN, :HD].reshape(held, HD)
            value_far[i * held : (i + 1) * held] = prompt[:, :OWN, HD:].reshape(held, HD)
        if first:
            key_sum[...] = jnp.zeros_like(key_sum)
            value_sum[...] = jnp.zeros_like(value_sum)
        else:
            key_sum[...] = far_in[0]
            value_sum[...] = far_in[1]

    row = lax.broadcasted_iota(jnp.int32, (ROWS, 1), 0)
    at = lax.broadcasted_iota(jnp.int32, (ROWS, ROWS), 0)
    of = lax.broadcasted_iota(jnp.int32, (ROWS, ROWS), 1)
    seen = (of <= at) & ((of // RESP_LEN) == (at // RESP_LEN))
    hide = jnp.concatenate([jnp.where(seen, 0.0, -1e30).astype(F32)] * per, 0)

    class Tile:
        pass

    tiles = []
    for source in range(PER_STEP):
        meta = prompts[0][step * PER_STEP + source, OWN:, :].astype(F32)
        order = one_hot_rows(meta[0:1, :HD].astype(jnp.int32))
        moved = dot(order, rows_ref[:, source].reshape(ROWS, -1), NN).astype(BF)
        if first:
            pair = moved[:, 2 * wide :]
        else:
            pair = dot(order, pair_ref[:, source].reshape(ROWS, -1), NN).astype(BF)
        count = jnp.where(
            row < RESP_LEN, meta[0:1, HD : HD + 1], meta[0:1, HD + 1 : HD + 2] + RESP_LEN
        )
        live = jnp.concatenate([(row.astype(F32) < count).astype(F32)] * per, 0)
        near = Tile()
        near.key, near.value = pair[:, :HD], pair[:, HD:]
        near.key_sum = jnp.zeros((HD, ROWS), F32) if first else near_in[source, 0]
        near.value_sum = jnp.zeros((HD, ROWS), F32) if first else near_in[source, 1]
        for part in range(parts):
            t = Tile()
            t.source, t.near, t.live, t.closes = source, near, live, part == parts - 1
            t.cols = [slice((part * per + a) * HD, (part * per + a + 1) * HD) for a in range(per)]
            t.query = jnp.concatenate([moved[:, c] for c in t.cols], 0)
            t.grad = jnp.concatenate([moved[:, wide + c.start : wide + c.stop] for c in t.cols], 0)
            odd = len(tiles) % 2
            t.expo, t.rounded = (expo_odd, rounded_odd) if odd else (expo_even, rounded_even)
            tiles.append(t)

    def score_near(t):
        t.score_near = dot(t.query, t.near.key, NT) + hide
        t.largest = t.score_near

    def score_far(t, b):
        score = dot(t.query, key_far[b], NT)
        t.expo[:, b] = score
        for j in lanes:
            t.largest = jnp.maximum(t.largest, score[:, j])

    def expo_near(t):
        t.shift = jnp.max(t.largest, axis=1, keepdims=True) * EXP_SCALE
        t.expo_near = jnp.exp2(t.score_near * EXP_SCALE - t.shift)
        t.total = t.expo_near

    def expo_far(t, b):
        value = jnp.exp2(t.expo[:, b] * EXP_SCALE - t.shift)
        t.expo[:, b] = value
        for j in lanes:
            t.total = t.total + value[:, j]

    def attend_near(t):
        t.factor = t.live / jnp.sum(t.total, axis=1, keepdims=True)
        t.rounded_near = (t.expo_near * t.factor).astype(BF)
        t.attended = dot(t.rounded_near, t.near.value, NN)

    def attend_far(t, b):
        weight = (t.expo[:, b] * t.factor).astype(BF)
        t.rounded[:, b] = weight
        t.attended = t.attended + dot(weight, value_far[b], NN)

    def slope_near(t):
        t.attended = t.attended.astype(BF)
        t.delta = jnp.sum(t.grad.astype(F32) * t.attended.astype(F32), axis=1, keepdims=True)
        t.scaled = t.factor * SCALE
        slope = t.expo_near * t.scaled * (dot(t.grad, t.near.value, NT) - t.delta)
        slope = slope.astype(BF)
        t.query_grad = dot(slope, t.near.key, NN)
        t.query_t, t.grad_t = t.query.T, t.grad.T
        t.near.key_sum = t.near.key_sum + dot(t.query_t, slope, NN)
        t.near.value_sum = t.near.value_sum + dot(t.grad_t, t.rounded_near, NN)

    def slope_far(t, b):
        slope = t.expo[:, b] * t.scaled * (dot(t.grad, value_far[b], NT) - t.delta)
        slope = slope.astype(BF)
        t.query_grad = t.query_grad + dot(slope, key_far[b], NN)
        key_sum[:, b] += dot(t.query_t, slope, NN)
        value_sum[:, b] += dot(t.grad_t, t.rounded[:, b], NN)

    def store(t):
        query_grad = t.query_grad.astype(BF)
        for a, c in enumerate(t.cols):
            own = slice(a * ROWS, (a + 1) * ROWS)
            out[t.source, :, c] = t.attended[own]
            out[t.source, :, wide + c.start : wide + c.stop] = query_grad[own]
        if t.closes and last:
            out[t.source, :, 2 * wide : 2 * wide + HD] = t.near.key_sum.T.astype(BF)
            out[t.source, :, 2 * wide + HD :] = t.near.value_sum.T.astype(BF)
        elif t.closes:
            near_out[t.source, 0] = t.near.key_sum
            near_out[t.source, 1] = t.near.value_sum

    score_near(tiles[0])
    for b in blocks:
        score_far(tiles[0], b)
    expo_near(tiles[0])
    for b in blocks:
        expo_far(tiles[0], b)
    for t, after in zip(tiles, tiles[1:] + [None]):
        attend_near(t)
        if after:
            score_near(after)
        for b in blocks:
            attend_far(t, b)
            if after:
                score_far(after, b)
        slope_near(t)
        if after:
            expo_near(after)
        for b in blocks:
            slope_far(t, b)
            if after:
                expo_far(after, b)
        store(t)

    @pl.when(step == KV_HEADS // PER_STEP - 1)
    def _():
        if last:
            for half, summed in ((slice(0, HD), key_sum), (slice(HD, 2 * HD), value_sum)):
                terms = summed[...].T.reshape(4, KV_HEADS, OWN, HD)
                far_own[:, :, half] = terms[0]
                for i in range(3):
                    far_sent[i][:, :, half] = terms[i + 1].astype(BF)
        else:
            far_out[0] = key_sum[...]
            far_out[1] = value_sum[...]


def attend(heads, first, last, prompts, rows, pair_rows, pair_lane, far, near):
    tile = min(TILE_ROWS, heads * ROWS)
    wide = 2 * heads * HD
    width_in = wide + (2 * HD if first else 0)
    width_out = wide + (2 * HD if last else 0)
    near_spec = pl.BlockSpec((PER_STEP, 2, HD, ROWS), lambda i: (i, 0, 0, 0))
    arrays = [rows, *prompts]
    specs = [pl.BlockSpec((4, PER_STEP, 32, width_in), lambda i: (0, i, 0, 0))]
    specs += [full((KV_HEADS, OWN + META, 2 * HD))] * 4
    if not first:
        arrays += [pair_rows, far, near]
        specs += [
            pl.BlockSpec((4, PER_STEP, 32, 2 * HD), lambda i: (0, i, 0, pair_lane)),
            full((2, HD, NPOS)),
            near_spec,
        ]
    shapes = [jax.ShapeDtypeStruct((KV_HEADS, ROWS, width_out), BF)]
    out_specs = [pl.BlockSpec((PER_STEP, ROWS, width_out), lambda i: (i, 0, 0))]
    if last:
        term = (KV_HEADS, OWN, 2 * HD)
        shapes += [jax.ShapeDtypeStruct(term, F32)] + [jax.ShapeDtypeStruct(term, BF)] * 3
        out_specs += [full(term)] * 4
    else:
        shapes.append(jax.ShapeDtypeStruct((2, HD, NPOS), F32))
        out_specs.append(full((2, HD, NPOS)))
        shapes.append(jax.ShapeDtypeStruct((KV_HEADS, 2, HD, ROWS), F32))
        out_specs.append(near_spec)
    return pl.pallas_call(
        functools.partial(attend_kernel, heads, first, last, tile),
        grid=(KV_HEADS // PER_STEP,),
        in_specs=specs,
        out_specs=out_specs,
        out_shape=shapes,
        scratch_shapes=[
            pltpu.VMEM((NPOS, HD), BF),
            pltpu.VMEM((NPOS, HD), BF),
            pltpu.VMEM((tile, NPOS), F32),
            pltpu.VMEM((tile, NPOS), F32),
            pltpu.VMEM((tile, NPOS), BF),
            pltpu.VMEM((tile, NPOS), BF),
            pltpu.VMEM((HD, NPOS), F32),
            pltpu.VMEM((HD, NPOS), F32),
        ],
        compiler_params=params(),
        name="attend",
    )(*arrays)


def unpack_kernel(heads, start, with_pair, filled, ref, *refs):
    outs, done = refs[filled:-1], refs[-1]
    wide = heads * HD
    moves = []
    for head in range(KV_HEADS):
        at = pl.ds((head * GROUP + start) * HD, wide)
        moves.append((ref.at[head, :, pl.ds(0, wide)], outs[0].at[:, at]))
        moves.append((ref.at[head, :, pl.ds(wide, wide)], outs[1].at[:, at]))
        if with_pair:
            for half in range(2):
                part = ref.at[head, :, pl.ds(2 * wide + half * HD, HD)]
                moves.append((part, outs[2].at[:, pl.ds((half * KV_HEADS + head) * HD, HD)]))
    copies = [pltpu.make_async_copy(a, b, done.at[i]) for i, (a, b) in enumerate(moves)]
    for copy in copies:
        copy.start()
    for copy in copies:
        copy.wait()


def unpack(heads, start, with_pair, array, filled):
    shapes = [jax.ShapeDtypeStruct((ROWS, KV_HEADS * GROUP * HD), BF)] * 2
    if with_pair:
        shapes.append(jax.ShapeDtypeStruct((ROWS, 2 * KV_HEADS * HD), BF))
    return pl.pallas_call(
        functools.partial(unpack_kernel, heads, start, with_pair, len(filled)),
        grid=(1,),
        in_specs=[full(array.shape)] + [pl.BlockSpec(memory_space=pl.ANY)] * len(filled),
        out_specs=[pl.BlockSpec(memory_space=pl.ANY)] * len(shapes),
        out_shape=shapes,
        scratch_shapes=[pltpu.SemaphoreType.DMA((4 * KV_HEADS,))],
        input_output_aliases={1 + i: i for i in range(len(filled))},
        compiler_params=params(),
        name="unpack",
    )(array, *filled)


def add_terms_kernel(own, *refs):
    out = refs[-1]
    summed = own[...]
    for term in refs[:-1]:
        summed = summed + term[...].astype(F32)
    out[...] = summed


def add_terms(own, terms):
    shape = (KV_HEADS, OWN, 2 * HD)
    return pl.pallas_call(
        add_terms_kernel,
        grid=(1,),
        in_specs=[full(shape)] * 4,
        out_specs=full(shape),
        out_shape=jax.ShapeDtypeStruct(shape, F32),
        compiler_params=params(),
        name="add_terms",
    )(own, *terms)


def place_terms_kernel(terms, out):
    for head in range(KV_HEADS):
        value_at = (KV_HEADS + head) * HD
        out[0, :, head * HD : (head + 1) * HD] = terms[head, :, :HD]
        out[0, :, value_at : value_at + HD] = terms[head, :, HD:]


def place_terms(terms):
    shape = (1, OWN, 2 * KV_HEADS * HD)
    return pl.pallas_call(
        place_terms_kernel,
        grid=(1,),
        in_specs=[full((KV_HEADS, OWN, 2 * HD))],
        out_specs=full(shape),
        out_shape=jax.ShapeDtypeStruct(shape, F32),
        compiler_params=params(),
        name="place_terms",
    )(terms)


def exchange(array, axes):
    return lax.all_to_all(array, axes, split_axis=0, concat_axis=0, tiled=True)


def shift_x(array, by):
    return lax.ppermute(array, "x", [(i, (i + by) % 4) for i in range(4)])


def per_device(roll_query, roll_keyval, roll_grad, prompt_keyval, lengths, send_rows, land_rows):
    prompt = exchange(pack_prompt(prompt_keyval[0], land_rows, lengths), ("yl", "z"))
    rows = []
    start = 0
    for heads in CHUNKS:
        rows.append(pack_rows(heads, start, start == 0, roll_query, roll_grad, roll_keyval, send_rows))
        start += heads
    rows[0], prompt = lax.optimization_barrier((rows[0], prompt))
    prompts = [prompt] + [shift_x(prompt, i) for i in range(1, 4)]
    received = []
    for packed in rows:
        if len(received) == 1:
            packed, prompts, received = lax.optimization_barrier((packed, prompts, received))
        packed = exchange(packed.reshape(32, 32, -1), ("grp", "yl", "z"))
        received.append(packed.reshape(4, KV_HEADS, 32, -1))
    returned = []
    carried = (None, None)
    for index, heads in enumerate(CHUNKS):
        last = index == len(CHUNKS) - 1
        results = attend(
            heads, index == 0, last, prompts, received[index], received[0], CHUNKS[0], *carried
        )
        carried = results[1:]
        if returned:
            results, earlier = lax.optimization_barrier((results, returned[-1]))
            returned[-1] = earlier
            carried = results[1:]
        returned.append(exchange(results[0], ("yl", "z")))
    terms = add_terms(carried[0], [shift_x(carried[i], -i) for i in range(1, 4)])
    filled = ()
    start = 0
    for index, heads in enumerate(CHUNKS):
        if index == len(CHUNKS) - 1:
            terms, filled, returned[-1] = lax.optimization_barrier((terms, filled, returned[-1]))
        filled = unpack(heads, start, index == len(CHUNKS) - 1, returned[index], filled[:2])
        start += heads
    prompt_grad = place_terms(exchange(terms, ("yl", "z")))
    return (*filled, prompt_grad)


def solution(mesh):
    mesh = Mesh(mesh.devices.reshape(4, 2, 4, 4), ("grp", "yl", "z", "x"))
    rows = P(("grp", "yl", "z", "x"), None)
    placed = P("grp", ("yl", "z", "x"), None)
    return jax.shard_map(
        per_device,
        mesh=mesh,
        in_specs=(rows, rows, rows, placed, P("grp", ("yl", "z", "x")), placed, placed),
        out_specs=(rows, rows, rows, placed),
        check_vma=False,
    )
```

```python
import functools
import math

import jax
import jax.numpy as jnp
from jax import lax
from jax.experimental import pallas as pl
from jax.experimental.pallas import tpu as pltpu
from jax.sharding import Mesh, PartitionSpec as P

KV_HEADS = 8
GROUP = 8
HD = 128
ROWS = 128
RESP_LEN = 64
NPOS = 2048
OWN = 64
META = 16
SCALE = 1.0 / math.sqrt(HD)
EXP_SCALE = SCALE * math.log2(math.e)
F32 = jnp.float32
BF = jnp.bfloat16
NN = ((1,), (0,))
NT = ((1,), (1,))

CHUNKS = (4, 4)
TILE_ROWS = 512
POS_BLOCK = 1024
PER_STEP = 4
VMEM = 65408 * 1024


def dot(a, b, dims):
    return lax.dot_general(a, b, (dims, ((), ())), preferred_element_type=F32)


def full(shape):
    return pl.BlockSpec(shape, lambda i: (0,) * len(shape))


def params():
    return pltpu.CompilerParams(dimension_semantics=("arbitrary",), vmem_limit_bytes=VMEM)


def one_hot_rows(picks):
    chosen = lax.broadcasted_iota(jnp.int32, (ROWS, ROWS), 0) == picks
    return jnp.transpose(chosen.astype(F32)).astype(BF)


def partner(place, slot, sign):
    turn = (place[1] + sign * (slot % 4) + 4) % 4
    return ((place[0] + slot // 4) % 2) * 4 + turn


def pack_prompt_kernel(place, prompt, land, lens, *outs):
    lane = lax.broadcasted_iota(jnp.int32, (META, HD), 1)
    counts = jnp.where(lane == 0, lens[:, 0:1], lens[:, 1:2]).astype(F32).astype(BF)
    rows = jnp.broadcast_to(land[0], (META, HD)).astype(F32).astype(BF)
    for slot, out in enumerate(outs):
        head = partner(place, slot, 1)
        out[:OWN, :HD] = prompt[:, pl.ds(pl.multiple_of(head * HD, HD), HD)]
        out[:OWN, HD:] = prompt[:, pl.ds(pl.multiple_of((KV_HEADS + head) * HD, HD), HD)]
        out[OWN:, :HD] = rows
        out[OWN:, HD:] = counts


def pack_prompt(place, prompt, land, lens):
    shape = (OWN + META, 2 * HD)
    return pl.pallas_call(
        pack_prompt_kernel,
        grid=(1,),
        in_specs=[
            pl.BlockSpec(memory_space=pltpu.SMEM),
            full((OWN, 2 * KV_HEADS * HD)),
            full((1, 1, ROWS)),
            full((1, 2)),
        ],
        out_specs=[full(shape)] * KV_HEADS,
        out_shape=[jax.ShapeDtypeStruct(shape, BF)] * KV_HEADS,
        compiler_params=params(),
        name="pack_prompt",
    )(place, prompt, land, lens)


def gather_prompt_kernel(place, *refs):
    out = refs[-1]
    for slot, piece in enumerate(refs[:-1]):
        out[partner(place, slot, -1)] = piece[...]


def gather_prompt(place, pieces):
    shape = (OWN + META, 2 * HD)
    return pl.pallas_call(
        gather_prompt_kernel,
        grid=(1,),
        in_specs=[pl.BlockSpec(memory_space=pltpu.SMEM)] + [full(shape)] * KV_HEADS,
        out_specs=full((KV_HEADS, *shape)),
        out_shape=jax.ShapeDtypeStruct((KV_HEADS, *shape), BF),
        compiler_params=params(),
        name="gather_prompt",
    )(place, *pieces)


def pack_rows_kernel(wide, per_step, send, *refs):
    out = refs[-1]
    order = one_hot_rows(send[0])
    for a in range(per_step):
        for ref, at in zip((refs[a], refs[per_step + a]), (0, wide)):
            moved = dot(order, ref[...], NN).astype(BF)
            out[:, a, :, at : at + wide] = moved.reshape(4, 32, wide)
        for ref, at in zip(refs[2 * per_step : -1], (2 * wide, 2 * wide + HD)):
            moved = dot(order, ref[:, a * HD : (a + 1) * HD], NN).astype(BF)
            out[:, a, :, at : at + HD] = moved.reshape(4, 32, HD)


def pack_rows(heads, start, with_pair, query, grad, pair, send):
    wide = heads * HD
    per = GROUP // heads
    first = start // heads
    per_step = 4
    steps = KV_HEADS // per_step
    specs = [full((1, 1, ROWS))]
    for _ in range(2):
        for a in range(per_step):
            specs.append(pl.BlockSpec((ROWS, wide), lambda i, a=a: (0, (i * per_step + a) * per + first)))
    arrays = [send] + [query] * per_step + [grad] * per_step
    width = 2 * wide
    if with_pair:
        specs += [
            pl.BlockSpec((ROWS, per_step * HD), lambda i: (0, i)),
            pl.BlockSpec((ROWS, per_step * HD), lambda i: (0, steps + i)),
        ]
        arrays += [pair, pair]
        width += 2 * HD
    return pl.pallas_call(
        functools.partial(pack_rows_kernel, wide, per_step),
        grid=(steps,),
        in_specs=specs,
        out_specs=pl.BlockSpec((4, per_step, 32, width), lambda i: (0, i, 0, 0)),
        out_shape=jax.ShapeDtypeStruct((4, KV_HEADS, 32, width), BF),
        compiler_params=params(),
        name="pack_rows",
    )(*arrays)


def attend_kernel(heads, first, last, tile, *refs):
    refs = list(refs)
    rows_ref, prompts = refs[0], refs[1:5]
    refs = refs[5:]
    if not first:
        pair_ref, far_in, near_in = refs[:3]
        refs = refs[3:]
    out = refs[0]
    if last:
        far_own, far_sent = refs[1], refs[2:5]
        refs = refs[5:]
    else:
        far_out, near_out = refs[1:3]
        refs = refs[3:]
    key_far, value_far, expo_even, expo_odd, rounded_even, rounded_odd, key_sum, value_sum = refs
    step = pl.program_id(0)
    wide = heads * HD
    held = KV_HEADS * OWN
    per = tile // ROWS
    parts = heads // per
    blocks = [slice(b, b + POS_BLOCK) for b in range(0, NPOS, POS_BLOCK)]
    lanes = [slice(j, j + HD) for j in range(0, POS_BLOCK, HD)]

    @pl.when(step == 0)
    def _():
        for i, prompt in enumerate(prompts):
            key_far[i * held : (i + 1) * held] = prompt[:, :OWN, :HD].reshape(held, HD)
            value_far[i * held : (i + 1) * held] = prompt[:, :OWN, HD:].reshape(held, HD)
        if first:
            key_sum[...] = jnp.zeros_like(key_sum)
            value_sum[...] = jnp.zeros_like(value_sum)
        else:
            key_sum[...] = far_in[0]
            value_sum[...] = far_in[1]

    row = lax.broadcasted_iota(jnp.int32, (ROWS, 1), 0)
    at = lax.broadcasted_iota(jnp.int32, (ROWS, ROWS), 0)
    of = lax.broadcasted_iota(jnp.int32, (ROWS, ROWS), 1)
    seen = (of <= at) & ((of // RESP_LEN) == (at // RESP_LEN))
    hide = jnp.concatenate([jnp.where(seen, 0.0, -1e30).astype(F32)] * per, 0)

    class Tile:
        pass

    tiles = []
    for source in range(PER_STEP):
        meta = prompts[0][step * PER_STEP + source, OWN:, :].astype(F32)
        order = one_hot_rows(meta[0:1, :HD].astype(jnp.int32))
        moved = dot(order, rows_ref[:, source].reshape(ROWS, -1), NN).astype(BF)
        if first:
            pair = moved[:, 2 * wide :]
        else:
            pair = dot(order, pair_ref[:, source].reshape(ROWS, -1), NN).astype(BF)
        count = jnp.where(
            row < RESP_LEN, meta[0:1, HD : HD + 1], meta[0:1, HD + 1 : HD + 2] + RESP_LEN
        )
        live = jnp.concatenate([(row.astype(F32) < count).astype(F32)] * per, 0)
        near = Tile()
        near.key, near.value = pair[:, :HD], pair[:, HD:]
        near.key_sum = jnp.zeros((HD, ROWS), F32) if first else near_in[source, 0]
        near.value_sum = jnp.zeros((HD, ROWS), F32) if first else near_in[source, 1]
        for part in range(parts):
            t = Tile()
            t.source, t.near, t.live, t.closes = source, near, live, part == parts - 1
            t.cols = [slice((part * per + a) * HD, (part * per + a + 1) * HD) for a in range(per)]
            t.query = jnp.concatenate([moved[:, c] for c in t.cols], 0)
            t.grad = jnp.concatenate([moved[:, wide + c.start : wide + c.stop] for c in t.cols], 0)
            odd = len(tiles) % 2
            t.expo, t.rounded = (expo_odd, rounded_odd) if odd else (expo_even, rounded_even)
            tiles.append(t)

    def score_near(t):
        t.score_near = dot(t.query, t.near.key, NT) + hide
        t.largest = t.score_near

    def score_far(t, b):
        score = dot(t.query, key_far[b], NT)
        t.expo[:, b] = score
        for j in lanes:
            t.largest = jnp.maximum(t.largest, score[:, j])

    def expo_near(t):
        t.shift = jnp.max(t.largest, axis=1, keepdims=True) * EXP_SCALE
        t.expo_near = jnp.exp2(t.score_near * EXP_SCALE - t.shift)
        t.total = t.expo_near

    def expo_far(t, b):
        value = jnp.exp2(t.expo[:, b] * EXP_SCALE - t.shift)
        t.expo[:, b] = value
        for j in lanes:
            t.total = t.total + value[:, j]

    def attend_near(t):
        t.factor = t.live / jnp.sum(t.total, axis=1, keepdims=True)
        t.rounded_near = (t.expo_near * t.factor).astype(BF)
        t.attended = dot(t.rounded_near, t.near.value, NN)

    def attend_far(t, b):
        weight = (t.expo[:, b] * t.factor).astype(BF)
        t.rounded[:, b] = weight
        t.attended = t.attended + dot(weight, value_far[b], NN)

    def slope_near(t):
        t.attended = t.attended.astype(BF)
        t.delta = jnp.sum(t.grad.astype(F32) * t.attended.astype(F32), axis=1, keepdims=True)
        t.scaled = t.factor * SCALE
        slope = t.expo_near * t.scaled * (dot(t.grad, t.near.value, NT) - t.delta)
        slope = slope.astype(BF)
        t.query_grad = dot(slope, t.near.key, NN)
        t.query_t, t.grad_t = t.query.T, t.grad.T
        t.near.key_sum = t.near.key_sum + dot(t.query_t, slope, NN)
        t.near.value_sum = t.near.value_sum + dot(t.grad_t, t.rounded_near, NN)

    def slope_far(t, b):
        slope = t.expo[:, b] * t.scaled * (dot(t.grad, value_far[b], NT) - t.delta)
        slope = slope.astype(BF)
        t.query_grad = t.query_grad + dot(slope, key_far[b], NN)
        key_sum[:, b] += dot(t.query_t, slope, NN)
        value_sum[:, b] += dot(t.grad_t, t.rounded[:, b], NN)

    def store(t):
        query_grad = t.query_grad.astype(BF)
        for a, c in enumerate(t.cols):
            own = slice(a * ROWS, (a + 1) * ROWS)
            out[t.source, :, c] = t.attended[own]
            out[t.source, :, wide + c.start : wide + c.stop] = query_grad[own]
        if t.closes and last:
            out[t.source, :, 2 * wide : 2 * wide + HD] = t.near.key_sum.T.astype(BF)
            out[t.source, :, 2 * wide + HD :] = t.near.value_sum.T.astype(BF)
        elif t.closes:
            near_out[t.source, 0] = t.near.key_sum
            near_out[t.source, 1] = t.near.value_sum

    score_near(tiles[0])
    for b in blocks:
        score_far(tiles[0], b)
    expo_near(tiles[0])
    for b in blocks:
        expo_far(tiles[0], b)
    for t, after in zip(tiles, tiles[1:] + [None]):
        attend_near(t)
        if after:
            score_near(after)
        for b in blocks:
            attend_far(t, b)
            if after:
                score_far(after, b)
        slope_near(t)
        if after:
            expo_near(after)
        for b in blocks:
            slope_far(t, b)
            if after:
                expo_far(after, b)
        store(t)

    @pl.when(step == KV_HEADS // PER_STEP - 1)
    def _():
        if last:
            for half, summed in ((slice(0, HD), key_sum), (slice(HD, 2 * HD), value_sum)):
                terms = summed[...].T.reshape(4, KV_HEADS, OWN, HD)
                far_own[:, :, half] = terms[0]
                for i in range(3):
                    far_sent[i][:, :, half] = terms[i + 1].astype(BF)
        else:
            far_out[0] = key_sum[...]
            far_out[1] = value_sum[...]


def attend(heads, first, last, prompts, rows, pair_rows, pair_lane, far, near):
    tile = min(TILE_ROWS, heads * ROWS)
    wide = 2 * heads * HD
    width_in = wide + (2 * HD if first else 0)
    width_out = wide + (2 * HD if last else 0)
    near_spec = pl.BlockSpec((PER_STEP, 2, HD, ROWS), lambda i: (i, 0, 0, 0))
    arrays = [rows, *prompts]
    specs = [pl.BlockSpec((4, PER_STEP, 32, width_in), lambda i: (0, i, 0, 0))]
    specs += [full((KV_HEADS, OWN + META, 2 * HD))] * 4
    if not first:
        arrays += [pair_rows, far, near]
        specs += [
            pl.BlockSpec((4, PER_STEP, 32, 2 * HD), lambda i: (0, i, 0, pair_lane)),
            full((2, HD, NPOS)),
            near_spec,
        ]
    shapes = [jax.ShapeDtypeStruct((KV_HEADS, ROWS, width_out), BF)]
    out_specs = [pl.BlockSpec((PER_STEP, ROWS, width_out), lambda i: (i, 0, 0))]
    if last:
        term = (KV_HEADS, OWN, 2 * HD)
        shapes += [jax.ShapeDtypeStruct(term, F32)] + [jax.ShapeDtypeStruct(term, BF)] * 3
        out_specs += [full(term)] * 4
    else:
        shapes.append(jax.ShapeDtypeStruct((2, HD, NPOS), F32))
        out_specs.append(full((2, HD, NPOS)))
        shapes.append(jax.ShapeDtypeStruct((KV_HEADS, 2, HD, ROWS), F32))
        out_specs.append(near_spec)
    return pl.pallas_call(
        functools.partial(attend_kernel, heads, first, last, tile),
        grid=(KV_HEADS // PER_STEP,),
        in_specs=specs,
        out_specs=out_specs,
        out_shape=shapes,
        scratch_shapes=[
            pltpu.VMEM((NPOS, HD), BF),
            pltpu.VMEM((NPOS, HD), BF),
            pltpu.VMEM((tile, NPOS), F32),
            pltpu.VMEM((tile, NPOS), F32),
            pltpu.VMEM((tile, NPOS), BF),
            pltpu.VMEM((tile, NPOS), BF),
            pltpu.VMEM((HD, NPOS), F32),
            pltpu.VMEM((HD, NPOS), F32),
        ],
        compiler_params=params(),
        name="attend",
    )(*arrays)


def unpack_kernel(heads, start, with_pair, filled, ref, *refs):
    outs, done = refs[filled:-1], refs[-1]
    wide = heads * HD
    moves = []
    for head in range(KV_HEADS):
        at = pl.ds((head * GROUP + start) * HD, wide)
        moves.append((ref.at[head, :, pl.ds(0, wide)], outs[0].at[:, at]))
        moves.append((ref.at[head, :, pl.ds(wide, wide)], outs[1].at[:, at]))
        if with_pair:
            for half in range(2):
                part = ref.at[head, :, pl.ds(2 * wide + half * HD, HD)]
                moves.append((part, outs[2].at[:, pl.ds((half * KV_HEADS + head) * HD, HD)]))
    copies = [pltpu.make_async_copy(a, b, done.at[i]) for i, (a, b) in enumerate(moves)]
    for copy in copies:
        copy.start()
    for copy in copies:
        copy.wait()


def unpack(heads, start, with_pair, array, filled):
    shapes = [jax.ShapeDtypeStruct((ROWS, KV_HEADS * GROUP * HD), BF)] * 2
    if with_pair:
        shapes.append(jax.ShapeDtypeStruct((ROWS, 2 * KV_HEADS * HD), BF))
    return pl.pallas_call(
        functools.partial(unpack_kernel, heads, start, with_pair, len(filled)),
        grid=(1,),
        in_specs=[full(array.shape)] + [pl.BlockSpec(memory_space=pl.ANY)] * len(filled),
        out_specs=[pl.BlockSpec(memory_space=pl.ANY)] * len(shapes),
        out_shape=shapes,
        scratch_shapes=[pltpu.SemaphoreType.DMA((4 * KV_HEADS,))],
        input_output_aliases={1 + i: i for i in range(len(filled))},
        compiler_params=params(),
        name="unpack",
    )(array, *filled)


def add_terms_kernel(place, own, *refs):
    terms, outs = refs[:3], refs[3:]
    for slot, out in enumerate(outs):
        head = partner(place, slot, 1)
        summed = own[head]
        for term in terms:
            summed = summed + term[head].astype(F32)
        out[...] = summed.astype(out.dtype)


def add_terms(place, own, terms):
    shape = (OWN, 2 * HD)
    kinds = [F32] + [BF] * (KV_HEADS - 1)
    return pl.pallas_call(
        add_terms_kernel,
        grid=(1,),
        in_specs=[pl.BlockSpec(memory_space=pltpu.SMEM)] + [full((KV_HEADS, *shape))] * 4,
        out_specs=[full(shape)] * KV_HEADS,
        out_shape=[jax.ShapeDtypeStruct(shape, kind) for kind in kinds],
        compiler_params=params(),
        name="add_terms",
    )(place, own, *terms)


def place_terms_kernel(place, *refs):
    out = refs[-1]
    for slot, term in enumerate(refs[:-1]):
        head = partner(place, slot, -1)
        key_at = pl.ds(pl.multiple_of(head * HD, HD), HD)
        value_at = pl.ds(pl.multiple_of((KV_HEADS + head) * HD, HD), HD)
        out[0, :, key_at] = term[:, :HD].astype(F32)
        out[0, :, value_at] = term[:, HD:].astype(F32)


def place_terms(place, terms):
    shape = (1, OWN, 2 * KV_HEADS * HD)
    return pl.pallas_call(
        place_terms_kernel,
        grid=(1,),
        in_specs=[pl.BlockSpec(memory_space=pltpu.SMEM)] + [full((OWN, 2 * HD))] * KV_HEADS,
        out_specs=full(shape),
        out_shape=jax.ShapeDtypeStruct(shape, F32),
        compiler_params=params(),
        name="place_terms",
    )(place, *terms)


def exchange(array, axes):
    return lax.all_to_all(array, axes, split_axis=0, concat_axis=0, tiled=True)


def shift_x(array, by):
    return lax.ppermute(array, "x", [(i, (i + by) % 4) for i in range(4)])


def shift_head(array, slot):
    pairs = []
    for yl in range(2):
        for z in range(4):
            there = ((yl + slot // 4) % 2) * 4 + (z + slot % 4) % 4
            pairs.append((yl * 4 + z, there))
    return lax.ppermute(array, ("yl", "z"), pairs)


def shift_heads(pieces):
    return [pieces[0]] + [shift_head(pieces[k], k) for k in range(1, KV_HEADS)]


def per_device(roll_query, roll_keyval, roll_grad, prompt_keyval, lengths, send_rows, land_rows):
    place = jnp.stack([lax.axis_index("yl"), lax.axis_index("z")]).astype(jnp.int32)
    pieces = shift_heads(pack_prompt(place, prompt_keyval[0], land_rows, lengths))
    prompt = gather_prompt(place, pieces)
    prompts = [prompt] + [shift_x(prompt, i) for i in range(1, 4)]
    rows = []
    start = 0
    for heads in CHUNKS:
        rows.append(pack_rows(heads, start, start == 0, roll_query, roll_grad, roll_keyval, send_rows))
        start += heads
    received = []
    for packed in rows:
        if len(received) == 1:
            packed, prompts, received = lax.optimization_barrier((packed, prompts, received))
        packed = exchange(packed.reshape(32, 32, -1), ("grp", "yl", "z"))
        received.append(packed.reshape(4, KV_HEADS, 32, -1))
    returned = []
    carried = (None, None)
    for index, heads in enumerate(CHUNKS):
        last = index == len(CHUNKS) - 1
        results = attend(
            heads, index == 0, last, prompts, received[index], received[0], CHUNKS[0], *carried
        )
        carried = results[1:]
        if returned:
            results, earlier = lax.optimization_barrier((results, returned[-1]))
            returned[-1] = earlier
            carried = results[1:]
        returned.append(exchange(results[0], ("yl", "z")))
    terms = add_terms(place, carried[0], [shift_x(carried[i], -i) for i in range(1, 4)])
    prompt_grad = place_terms(place, shift_heads(terms))
    filled = ()
    start = 0
    for index, heads in enumerate(CHUNKS):
        if index == len(CHUNKS) - 1:
            filled, returned[-1] = lax.optimization_barrier((filled, returned[-1]))
        filled = unpack(heads, start, index == len(CHUNKS) - 1, returned[index], filled[:2])
        start += heads
    return (*filled, prompt_grad)


def solution(mesh):
    mesh = Mesh(mesh.devices.reshape(4, 2, 4, 4), ("grp", "yl", "z", "x"))
    rows = P(("grp", "yl", "z", "x"), None)
    placed = P("grp", ("yl", "z", "x"), None)
    return jax.shard_map(
        per_device,
        mesh=mesh,
        in_specs=(rows, rows, rows, placed, P("grp", ("yl", "z", "x")), placed, placed),
        out_specs=(rows, rows, rows, placed),
        check_vma=False,
    )
```

```python
import functools
import math

import jax
import jax.numpy as jnp
from jax import lax
from jax.experimental import pallas as pl
from jax.experimental.pallas import tpu as pltpu
from jax.sharding import Mesh, PartitionSpec as P

KV_HEADS = 8
GROUP = 8
HD = 128
ROWS = 128
RESP_LEN = 64
NPOS = 2048
OWN = 64
META = 16
SCALE = 1.0 / math.sqrt(HD)
EXP_SCALE = SCALE * math.log2(math.e)
F32 = jnp.float32
BF = jnp.bfloat16
NN = ((1,), (0,))
NT = ((1,), (1,))

CHUNKS = (4, 4)
TILE_ROWS = 512
POS_BLOCK = 1024
PER_STEP = 4
VMEM = 65408 * 1024


def dot(a, b, dims):
    return lax.dot_general(a, b, (dims, ((), ())), preferred_element_type=F32)


def full(shape):
    return pl.BlockSpec(shape, lambda i: (0,) * len(shape))


def params():
    return pltpu.CompilerParams(dimension_semantics=("arbitrary",), vmem_limit_bytes=VMEM)


def one_hot_rows(picks):
    chosen = lax.broadcasted_iota(jnp.int32, (ROWS, ROWS), 0) == picks
    return jnp.transpose(chosen.astype(F32)).astype(BF)


def partner(place, slot, sign):
    turn = (place[1] + sign * (slot % 4) + 4) % 4
    return ((place[0] + slot // 4) % 2) * 4 + turn


def pack_prompt_kernel(prompt, land, lens, out):
    lane = lax.broadcasted_iota(jnp.int32, (META, HD), 1)
    counts = jnp.where(lane == 0, lens[:, 0:1], lens[:, 1:2]).astype(F32).astype(BF)
    rows = jnp.broadcast_to(land[0], (META, HD)).astype(F32).astype(BF)
    for head in range(KV_HEADS):
        value_at = (KV_HEADS + head) * HD
        out[head, :OWN, :HD] = prompt[:, head * HD : (head + 1) * HD]
        out[head, :OWN, HD:] = prompt[:, value_at : value_at + HD]
        out[head, OWN:, :HD] = rows
        out[head, OWN:, HD:] = counts


def pack_prompt(prompt, land, lens):
    shape = (KV_HEADS, OWN + META, 2 * HD)
    return pl.pallas_call(
        pack_prompt_kernel,
        grid=(1,),
        in_specs=[full((OWN, 2 * KV_HEADS * HD)), full((1, 1, ROWS)), full((1, 2))],
        out_specs=full(shape),
        out_shape=jax.ShapeDtypeStruct(shape, BF),
        compiler_params=params(),
        name="pack_prompt",
    )(prompt, land, lens)


def pack_rows_kernel(wide, per_step, send, *refs):
    out = refs[-1]
    order = one_hot_rows(send[0])
    for a in range(per_step):
        for ref, at in zip((refs[a], refs[per_step + a]), (0, wide)):
            moved = dot(order, ref[...], NN).astype(BF)
            out[:, a, :, at : at + wide] = moved.reshape(4, 32, wide)
        for ref, at in zip(refs[2 * per_step : -1], (2 * wide, 2 * wide + HD)):
            moved = dot(order, ref[:, a * HD : (a + 1) * HD], NN).astype(BF)
            out[:, a, :, at : at + HD] = moved.reshape(4, 32, HD)


def pack_rows(heads, start, with_pair, query, grad, pair, send):
    wide = heads * HD
    per = GROUP // heads
    first = start // heads
    per_step = 4
    steps = KV_HEADS // per_step
    specs = [full((1, 1, ROWS))]
    for _ in range(2):
        for a in range(per_step):
            specs.append(pl.BlockSpec((ROWS, wide), lambda i, a=a: (0, (i * per_step + a) * per + first)))
    arrays = [send] + [query] * per_step + [grad] * per_step
    width = 2 * wide
    if with_pair:
        specs += [
            pl.BlockSpec((ROWS, per_step * HD), lambda i: (0, i)),
            pl.BlockSpec((ROWS, per_step * HD), lambda i: (0, steps + i)),
        ]
        arrays += [pair, pair]
        width += 2 * HD
    return pl.pallas_call(
        functools.partial(pack_rows_kernel, wide, per_step),
        grid=(steps,),
        in_specs=specs,
        out_specs=pl.BlockSpec((4, per_step, 32, width), lambda i: (0, i, 0, 0)),
        out_shape=jax.ShapeDtypeStruct((4, KV_HEADS, 32, width), BF),
        compiler_params=params(),
        name="pack_rows",
    )(*arrays)


def attend_kernel(heads, first, last, tile, *refs):
    refs = list(refs)
    rows_ref, prompts = refs[0], refs[1:5]
    refs = refs[5:]
    if not first:
        pair_ref, far_in, near_in = refs[:3]
        refs = refs[3:]
    out = refs[0]
    if last:
        far_own, far_sent = refs[1], refs[2:5]
        refs = refs[5:]
    else:
        far_out, near_out = refs[1:3]
        refs = refs[3:]
    key_far, value_far, expo_even, expo_odd, rounded_even, rounded_odd, key_sum, value_sum = refs
    step = pl.program_id(0)
    wide = heads * HD
    held = KV_HEADS * OWN
    per = tile // ROWS
    parts = heads // per
    blocks = [slice(b, b + POS_BLOCK) for b in range(0, NPOS, POS_BLOCK)]
    lanes = [slice(j, j + HD) for j in range(0, POS_BLOCK, HD)]

    @pl.when(step == 0)
    def _():
        for i, prompt in enumerate(prompts):
            key_far[i * held : (i + 1) * held] = prompt[:, :OWN, :HD].reshape(held, HD)
            value_far[i * held : (i + 1) * held] = prompt[:, :OWN, HD:].reshape(held, HD)
        if first:
            key_sum[...] = jnp.zeros_like(key_sum)
            value_sum[...] = jnp.zeros_like(value_sum)
        else:
            key_sum[...] = far_in[0]
            value_sum[...] = far_in[1]

    row = lax.broadcasted_iota(jnp.int32, (ROWS, 1), 0)
    at = lax.broadcasted_iota(jnp.int32, (ROWS, ROWS), 0)
    of = lax.broadcasted_iota(jnp.int32, (ROWS, ROWS), 1)
    seen = (of <= at) & ((of // RESP_LEN) == (at // RESP_LEN))
    hide = jnp.concatenate([jnp.where(seen, 0.0, -1e30).astype(F32)] * per, 0)

    class Tile:
        pass

    tiles = []
    for source in range(PER_STEP):
        meta = prompts[0][step * PER_STEP + source, OWN:, :].astype(F32)
        order = one_hot_rows(meta[0:1, :HD].astype(jnp.int32))
        moved = dot(order, rows_ref[:, source].reshape(ROWS, -1), NN).astype(BF)
        if first:
            pair = moved[:, 2 * wide :]
        else:
            pair = dot(order, pair_ref[:, source].reshape(ROWS, -1), NN).astype(BF)
        count = jnp.where(
            row < RESP_LEN, meta[0:1, HD : HD + 1], meta[0:1, HD + 1 : HD + 2] + RESP_LEN
        )
        live = jnp.concatenate([(row.astype(F32) < count).astype(F32)] * per, 0)
        near = Tile()
        near.key, near.value = pair[:, :HD], pair[:, HD:]
        near.key_sum = jnp.zeros((HD, ROWS), F32) if first else near_in[source, 0]
        near.value_sum = jnp.zeros((HD, ROWS), F32) if first else near_in[source, 1]
        for part in range(parts):
            t = Tile()
            t.source, t.near, t.live, t.closes = source, near, live, part == parts - 1
            t.cols = [slice((part * per + a) * HD, (part * per + a + 1) * HD) for a in range(per)]
            t.query = jnp.concatenate([moved[:, c] for c in t.cols], 0)
            t.grad = jnp.concatenate([moved[:, wide + c.start : wide + c.stop] for c in t.cols], 0)
            odd = len(tiles) % 2
            t.expo, t.rounded = (expo_odd, rounded_odd) if odd else (expo_even, rounded_even)
            tiles.append(t)

    def score_near(t):
        t.score_near = dot(t.query, t.near.key, NT) + hide
        t.largest = t.score_near

    def score_far(t, b):
        score = dot(t.query, key_far[b], NT)
        t.expo[:, b] = score
        for j in lanes:
            t.largest = jnp.maximum(t.largest, score[:, j])

    def expo_near(t):
        t.shift = jnp.max(t.largest, axis=1, keepdims=True) * EXP_SCALE
        t.expo_near = jnp.exp2(t.score_near * EXP_SCALE - t.shift)
        t.total = t.expo_near

    def expo_far(t, b):
        value = jnp.exp2(t.expo[:, b] * EXP_SCALE - t.shift)
        t.expo[:, b] = value
        for j in lanes:
            t.total = t.total + value[:, j]

    def attend_near(t):
        t.factor = t.live / jnp.sum(t.total, axis=1, keepdims=True)
        t.rounded_near = (t.expo_near * t.factor).astype(BF)
        t.attended = dot(t.rounded_near, t.near.value, NN)

    def attend_far(t, b):
        weight = (t.expo[:, b] * t.factor).astype(BF)
        t.rounded[:, b] = weight
        t.attended = t.attended + dot(weight, value_far[b], NN)

    def slope_near(t):
        t.attended = t.attended.astype(BF)
        t.delta = jnp.sum(t.grad.astype(F32) * t.attended.astype(F32), axis=1, keepdims=True)
        t.scaled = t.factor * SCALE
        slope = t.expo_near * t.scaled * (dot(t.grad, t.near.value, NT) - t.delta)
        slope = slope.astype(BF)
        t.query_grad = dot(slope, t.near.key, NN)
        t.query_t, t.grad_t = t.query.T, t.grad.T
        t.near.key_sum = t.near.key_sum + dot(t.query_t, slope, NN)
        t.near.value_sum = t.near.value_sum + dot(t.grad_t, t.rounded_near, NN)

    def slope_far(t, b):
        slope = t.expo[:, b] * t.scaled * (dot(t.grad, value_far[b], NT) - t.delta)
        slope = slope.astype(BF)
        t.query_grad = t.query_grad + dot(slope, key_far[b], NN)
        key_sum[:, b] += dot(t.query_t, slope, NN)
        value_sum[:, b] += dot(t.grad_t, t.rounded[:, b], NN)

    def store(t):
        query_grad = t.query_grad.astype(BF)
        for a, c in enumerate(t.cols):
            own = slice(a * ROWS, (a + 1) * ROWS)
            out[t.source, :, c] = t.attended[own]
            out[t.source, :, wide + c.start : wide + c.stop] = query_grad[own]
        if t.closes and last:
            out[t.source, :, 2 * wide : 2 * wide + HD] = t.near.key_sum.T.astype(BF)
            out[t.source, :, 2 * wide + HD :] = t.near.value_sum.T.astype(BF)
        elif t.closes:
            near_out[t.source, 0] = t.near.key_sum
            near_out[t.source, 1] = t.near.value_sum

    score_near(tiles[0])
    for b in blocks:
        score_far(tiles[0], b)
    expo_near(tiles[0])
    for b in blocks:
        expo_far(tiles[0], b)
    for t, after in zip(tiles, tiles[1:] + [None]):
        attend_near(t)
        if after:
            score_near(after)
        for b in blocks:
            attend_far(t, b)
            if after:
                score_far(after, b)
        slope_near(t)
        if after:
            expo_near(after)
        for b in blocks:
            slope_far(t, b)
            if after:
                expo_far(after, b)
        store(t)

    @pl.when(step == KV_HEADS // PER_STEP - 1)
    def _():
        if last:
            for half, summed in ((slice(0, HD), key_sum), (slice(HD, 2 * HD), value_sum)):
                terms = summed[...].T.reshape(4, KV_HEADS, OWN, HD)
                far_own[:, :, half] = terms[0]
                for i in range(3):
                    far_sent[i][:, :, half] = terms[i + 1].astype(BF)
        else:
            far_out[0] = key_sum[...]
            far_out[1] = value_sum[...]


def attend(heads, first, last, prompts, rows, pair_rows, pair_lane, far, near):
    tile = min(TILE_ROWS, heads * ROWS)
    wide = 2 * heads * HD
    width_in = wide + (2 * HD if first else 0)
    width_out = wide + (2 * HD if last else 0)
    near_spec = pl.BlockSpec((PER_STEP, 2, HD, ROWS), lambda i: (i, 0, 0, 0))
    arrays = [rows, *prompts]
    specs = [pl.BlockSpec((4, PER_STEP, 32, width_in), lambda i: (0, i, 0, 0))]
    specs += [full((KV_HEADS, OWN + META, 2 * HD))] * 4
    if not first:
        arrays += [pair_rows, far, near]
        specs += [
            pl.BlockSpec((4, PER_STEP, 32, 2 * HD), lambda i: (0, i, 0, pair_lane)),
            full((2, HD, NPOS)),
            near_spec,
        ]
    shapes = [jax.ShapeDtypeStruct((KV_HEADS, ROWS, width_out), BF)]
    out_specs = [pl.BlockSpec((PER_STEP, ROWS, width_out), lambda i: (i, 0, 0))]
    if last:
        term = (KV_HEADS, OWN, 2 * HD)
        shapes += [jax.ShapeDtypeStruct(term, F32)] + [jax.ShapeDtypeStruct(term, BF)] * 3
        out_specs += [full(term)] * 4
    else:
        shapes.append(jax.ShapeDtypeStruct((2, HD, NPOS), F32))
        out_specs.append(full((2, HD, NPOS)))
        shapes.append(jax.ShapeDtypeStruct((KV_HEADS, 2, HD, ROWS), F32))
        out_specs.append(near_spec)
    return pl.pallas_call(
        functools.partial(attend_kernel, heads, first, last, tile),
        grid=(KV_HEADS // PER_STEP,),
        in_specs=specs,
        out_specs=out_specs,
        out_shape=shapes,
        scratch_shapes=[
            pltpu.VMEM((NPOS, HD), BF),
            pltpu.VMEM((NPOS, HD), BF),
            pltpu.VMEM((tile, NPOS), F32),
            pltpu.VMEM((tile, NPOS), F32),
            pltpu.VMEM((tile, NPOS), BF),
            pltpu.VMEM((tile, NPOS), BF),
            pltpu.VMEM((HD, NPOS), F32),
            pltpu.VMEM((HD, NPOS), F32),
        ],
        compiler_params=params(),
        name="attend",
    )(*arrays)


def unpack_kernel(heads, start, with_pair, filled, ref, *refs):
    outs, done = refs[filled:-1], refs[-1]
    wide = heads * HD
    moves = []
    for head in range(KV_HEADS):
        at = pl.ds((head * GROUP + start) * HD, wide)
        moves.append((ref.at[head, :, pl.ds(0, wide)], outs[0].at[:, at]))
        moves.append((ref.at[head, :, pl.ds(wide, wide)], outs[1].at[:, at]))
        if with_pair:
            for half in range(2):
                part = ref.at[head, :, pl.ds(2 * wide + half * HD, HD)]
                moves.append((part, outs[2].at[:, pl.ds((half * KV_HEADS + head) * HD, HD)]))
    copies = [pltpu.make_async_copy(a, b, done.at[i]) for i, (a, b) in enumerate(moves)]
    for copy in copies:
        copy.start()
    for copy in copies:
        copy.wait()


def unpack(heads, start, with_pair, array, filled):
    shapes = [jax.ShapeDtypeStruct((ROWS, KV_HEADS * GROUP * HD), BF)] * 2
    if with_pair:
        shapes.append(jax.ShapeDtypeStruct((ROWS, 2 * KV_HEADS * HD), BF))
    return pl.pallas_call(
        functools.partial(unpack_kernel, heads, start, with_pair, len(filled)),
        grid=(1,),
        in_specs=[full(array.shape)] + [pl.BlockSpec(memory_space=pl.ANY)] * len(filled),
        out_specs=[pl.BlockSpec(memory_space=pl.ANY)] * len(shapes),
        out_shape=shapes,
        scratch_shapes=[pltpu.SemaphoreType.DMA((4 * KV_HEADS,))],
        input_output_aliases={1 + i: i for i in range(len(filled))},
        compiler_params=params(),
        name="unpack",
    )(array, *filled)


def add_terms_kernel(place, own, *refs):
    terms, outs = refs[:3], refs[3:]
    for slot, out in enumerate(outs):
        head = partner(place, slot, 1)
        summed = own[head]
        for term in terms:
            summed = summed + term[head].astype(F32)
        out[...] = summed.astype(out.dtype)


def add_terms(place, own, terms):
    shape = (OWN, 2 * HD)
    kinds = [F32] + [BF] * (KV_HEADS - 1)
    return pl.pallas_call(
        add_terms_kernel,
        grid=(1,),
        in_specs=[pl.BlockSpec(memory_space=pltpu.SMEM)] + [full((KV_HEADS, *shape))] * 4,
        out_specs=[full(shape)] * KV_HEADS,
        out_shape=[jax.ShapeDtypeStruct(shape, kind) for kind in kinds],
        compiler_params=params(),
        name="add_terms",
    )(place, own, *terms)


def place_terms_kernel(place, *refs):
    out = refs[-1]
    for slot, term in enumerate(refs[:-1]):
        head = partner(place, slot, -1)
        key_at = pl.ds(pl.multiple_of(head * HD, HD), HD)
        value_at = pl.ds(pl.multiple_of((KV_HEADS + head) * HD, HD), HD)
        out[0, :, key_at] = term[:, :HD].astype(F32)
        out[0, :, value_at] = term[:, HD:].astype(F32)


def place_terms(place, terms):
    shape = (1, OWN, 2 * KV_HEADS * HD)
    return pl.pallas_call(
        place_terms_kernel,
        grid=(1,),
        in_specs=[pl.BlockSpec(memory_space=pltpu.SMEM)] + [full((OWN, 2 * HD))] * KV_HEADS,
        out_specs=full(shape),
        out_shape=jax.ShapeDtypeStruct(shape, F32),
        compiler_params=params(),
        name="place_terms",
    )(place, *terms)


def exchange(array, axes):
    return lax.all_to_all(array, axes, split_axis=0, concat_axis=0, tiled=True)


def shift_x(array, by):
    return lax.ppermute(array, "x", [(i, (i + by) % 4) for i in range(4)])


def shift_head(array, slot):
    pairs = []
    for yl in range(2):
        for z in range(4):
            there = ((yl + slot // 4) % 2) * 4 + (z + slot % 4) % 4
            pairs.append((yl * 4 + z, there))
    return lax.ppermute(array, ("yl", "z"), pairs)


def shift_heads(pieces):
    return [pieces[0]] + [shift_head(pieces[k], k) for k in range(1, KV_HEADS)]


def per_device(roll_query, roll_keyval, roll_grad, prompt_keyval, lengths, send_rows, land_rows):
    place = jnp.stack([lax.axis_index("yl"), lax.axis_index("z")]).astype(jnp.int32)
    prompt = exchange(pack_prompt(prompt_keyval[0], land_rows, lengths), ("yl", "z"))
    rows = []
    start = 0
    for heads in CHUNKS:
        rows.append(pack_rows(heads, start, start == 0, roll_query, roll_grad, roll_keyval, send_rows))
        start += heads
    rows[0], prompt = lax.optimization_barrier((rows[0], prompt))
    prompts = [prompt] + [shift_x(prompt, i) for i in range(1, 4)]
    received = []
    for packed in rows:
        if len(received) == 1:
            packed, prompts, received = lax.optimization_barrier((packed, prompts, received))
        packed = exchange(packed.reshape(32, 32, -1), ("grp", "yl", "z"))
        received.append(packed.reshape(4, KV_HEADS, 32, -1))
    returned = []
    carried = (None, None)
    for index, heads in enumerate(CHUNKS):
        last = index == len(CHUNKS) - 1
        results = attend(
            heads, index == 0, last, prompts, received[index], received[0], CHUNKS[0], *carried
        )
        carried = results[1:]
        if returned:
            results, earlier = lax.optimization_barrier((results, returned[-1]))
            returned[-1] = earlier
            carried = results[1:]
        returned.append(exchange(results[0], ("yl", "z")))
    terms = [shift_x(carried[i], -i) for i in range(1, 4)]
    filled = ()
    start = 0
    for index, heads in enumerate(CHUNKS):
        last = index == len(CHUNKS) - 1
        if last:
            terms, filled = lax.optimization_barrier((terms, filled))
        filled = unpack(heads, start, last, returned[index], filled[:2])
        start += heads
    terms = shift_heads(add_terms(place, carried[0], terms))
    terms, filled = lax.optimization_barrier((terms, filled))
    return (*filled, place_terms(place, terms))


def solution(mesh):
    mesh = Mesh(mesh.devices.reshape(4, 2, 4, 4), ("grp", "yl", "z", "x"))
    rows = P(("grp", "yl", "z", "x"), None)
    placed = P("grp", ("yl", "z", "x"), None)
    return jax.shard_map(
        per_device,
        mesh=mesh,
        in_specs=(rows, rows, rows, placed, P("grp", ("yl", "z", "x")), placed, placed),
        out_specs=(rows, rows, rows, placed),
        check_vma=False,
    )
```

```python
import functools
import math

import jax
import jax.numpy as jnp
from jax import lax
from jax.experimental import pallas as pl
from jax.experimental.pallas import tpu as pltpu
from jax.sharding import Mesh, PartitionSpec as P

KV_HEADS = 8
GROUP = 8
HD = 128
ROWS = 128
RESP_LEN = 64
NPOS = 2048
OWN = 64
META = 16
SCALE = 1.0 / math.sqrt(HD)
EXP_SCALE = SCALE * math.log2(math.e)
F32 = jnp.float32
BF = jnp.bfloat16
NN = ((1,), (0,))
NT = ((1,), (1,))

CHUNKS = (4, 4)
TILE_ROWS = 512
POS_BLOCK = 1024
PER_STEP = 4
VMEM = 65408 * 1024


def dot(a, b, dims):
    return lax.dot_general(a, b, (dims, ((), ())), preferred_element_type=F32)


def full(shape):
    return pl.BlockSpec(shape, lambda i: (0,) * len(shape))


def params():
    return pltpu.CompilerParams(dimension_semantics=("arbitrary",), vmem_limit_bytes=VMEM)


def one_hot_rows(picks):
    chosen = lax.broadcasted_iota(jnp.int32, (ROWS, ROWS), 0) == picks
    return jnp.transpose(chosen.astype(F32)).astype(BF)


def partner(place, slot, sign):
    turn = (place[1] + sign * (slot % 4) + 4) % 4
    return ((place[0] + slot // 4) % 2) * 4 + turn


def pack_prompt_kernel(prompt, land, lens, out):
    lane = lax.broadcasted_iota(jnp.int32, (META, HD), 1)
    counts = jnp.where(lane == 0, lens[:, 0:1], lens[:, 1:2]).astype(F32).astype(BF)
    rows = jnp.broadcast_to(land[0], (META, HD)).astype(F32).astype(BF)
    for head in range(KV_HEADS):
        value_at = (KV_HEADS + head) * HD
        out[head, :OWN, :HD] = prompt[:, head * HD : (head + 1) * HD]
        out[head, :OWN, HD:] = prompt[:, value_at : value_at + HD]
        out[head, OWN:, :HD] = rows
        out[head, OWN:, HD:] = counts


def pack_prompt(prompt, land, lens):
    shape = (KV_HEADS, OWN + META, 2 * HD)
    return pl.pallas_call(
        pack_prompt_kernel,
        grid=(1,),
        in_specs=[full((OWN, 2 * KV_HEADS * HD)), full((1, 1, ROWS)), full((1, 2))],
        out_specs=full(shape),
        out_shape=jax.ShapeDtypeStruct(shape, BF),
        compiler_params=params(),
        name="pack_prompt",
    )(prompt, land, lens)


def pack_rows_kernel(wide, per_step, send, *refs):
    out = refs[-1]
    order = one_hot_rows(send[0])
    for a in range(per_step):
        for ref, at in zip((refs[a], refs[per_step + a]), (0, wide)):
            moved = dot(order, ref[...], NN).astype(BF)
            out[:, a, :, at : at + wide] = moved.reshape(4, 32, wide)
        for ref, at in zip(refs[2 * per_step : -1], (2 * wide, 2 * wide + HD)):
            moved = dot(order, ref[:, a * HD : (a + 1) * HD], NN).astype(BF)
            out[:, a, :, at : at + HD] = moved.reshape(4, 32, HD)


def pack_rows(heads, start, with_pair, query, grad, pair, send):
    wide = heads * HD
    per = GROUP // heads
    first = start // heads
    per_step = 4
    steps = KV_HEADS // per_step
    specs = [full((1, 1, ROWS))]
    for _ in range(2):
        for a in range(per_step):
            specs.append(pl.BlockSpec((ROWS, wide), lambda i, a=a: (0, (i * per_step + a) * per + first)))
    arrays = [send] + [query] * per_step + [grad] * per_step
    width = 2 * wide
    if with_pair:
        specs += [
            pl.BlockSpec((ROWS, per_step * HD), lambda i: (0, i)),
            pl.BlockSpec((ROWS, per_step * HD), lambda i: (0, steps + i)),
        ]
        arrays += [pair, pair]
        width += 2 * HD
    return pl.pallas_call(
        functools.partial(pack_rows_kernel, wide, per_step),
        grid=(steps,),
        in_specs=specs,
        out_specs=pl.BlockSpec((4, per_step, 32, width), lambda i: (0, i, 0, 0)),
        out_shape=jax.ShapeDtypeStruct((4, KV_HEADS, 32, width), BF),
        compiler_params=params(),
        name="pack_rows",
    )(*arrays)


def attend_kernel(heads, first, last, tile, *refs):
    refs = list(refs)
    rows_ref, prompts = refs[0], refs[1:5]
    refs = refs[5:]
    if not first:
        pair_ref, far_in, near_in = refs[:3]
        refs = refs[3:]
    out = refs[0]
    if last:
        far_own, far_sent = refs[1], refs[2:5]
        refs = refs[5:]
    else:
        far_out, near_out = refs[1:3]
        refs = refs[3:]
    key_far, value_far, expo_even, expo_odd, rounded_even, rounded_odd, key_sum, value_sum = refs
    step = pl.program_id(0)
    wide = heads * HD
    held = KV_HEADS * OWN
    per = tile // ROWS
    parts = heads // per
    blocks = [slice(b, b + POS_BLOCK) for b in range(0, NPOS, POS_BLOCK)]
    lanes = [slice(j, j + HD) for j in range(0, POS_BLOCK, HD)]

    @pl.when(step == 0)
    def _():
        for i, prompt in enumerate(prompts):
            key_far[i * held : (i + 1) * held] = prompt[:, :OWN, :HD].reshape(held, HD)
            value_far[i * held : (i + 1) * held] = prompt[:, :OWN, HD:].reshape(held, HD)
        if first:
            key_sum[...] = jnp.zeros_like(key_sum)
            value_sum[...] = jnp.zeros_like(value_sum)
        else:
            key_sum[...] = far_in[0]
            value_sum[...] = far_in[1]

    row = lax.broadcasted_iota(jnp.int32, (ROWS, 1), 0)
    at = lax.broadcasted_iota(jnp.int32, (ROWS, ROWS), 0)
    of = lax.broadcasted_iota(jnp.int32, (ROWS, ROWS), 1)
    seen = (of <= at) & ((of // RESP_LEN) == (at // RESP_LEN))
    hide = jnp.concatenate([jnp.where(seen, 0.0, -1e30).astype(F32)] * per, 0)

    class Tile:
        pass

    tiles = []
    for source in range(PER_STEP):
        meta = prompts[0][step * PER_STEP + source, OWN:, :].astype(F32)
        order = one_hot_rows(meta[0:1, :HD].astype(jnp.int32))
        moved = dot(order, rows_ref[:, source].reshape(ROWS, -1), NN).astype(BF)
        if first:
            pair = moved[:, 2 * wide :]
        else:
            pair = dot(order, pair_ref[:, source].reshape(ROWS, -1), NN).astype(BF)
        count = jnp.where(
            row < RESP_LEN, meta[0:1, HD : HD + 1], meta[0:1, HD + 1 : HD + 2] + RESP_LEN
        )
        live = jnp.concatenate([(row.astype(F32) < count).astype(F32)] * per, 0)
        near = Tile()
        near.key, near.value = pair[:, :HD], pair[:, HD:]
        near.key_sum = jnp.zeros((HD, ROWS), F32) if first else near_in[source, 0]
        near.value_sum = jnp.zeros((HD, ROWS), F32) if first else near_in[source, 1]
        for part in range(parts):
            t = Tile()
            t.source, t.near, t.live, t.closes = source, near, live, part == parts - 1
            t.cols = [slice((part * per + a) * HD, (part * per + a + 1) * HD) for a in range(per)]
            t.query = jnp.concatenate([moved[:, c] for c in t.cols], 0)
            t.grad = jnp.concatenate([moved[:, wide + c.start : wide + c.stop] for c in t.cols], 0)
            odd = len(tiles) % 2
            t.expo, t.rounded = (expo_odd, rounded_odd) if odd else (expo_even, rounded_even)
            tiles.append(t)

    def score_near(t):
        t.score_near = dot(t.query, t.near.key, NT) + hide
        t.largest = t.score_near

    def score_far(t, b):
        score = dot(t.query, key_far[b], NT)
        t.expo[:, b] = score
        for j in lanes:
            t.largest = jnp.maximum(t.largest, score[:, j])

    def expo_near(t):
        t.shift = jnp.max(t.largest, axis=1, keepdims=True) * EXP_SCALE
        t.expo_near = jnp.exp2(t.score_near * EXP_SCALE - t.shift)
        t.total = t.expo_near

    def expo_far(t, b):
        value = jnp.exp2(t.expo[:, b] * EXP_SCALE - t.shift)
        t.expo[:, b] = value
        for j in lanes:
            t.total = t.total + value[:, j]

    def attend_near(t):
        t.factor = t.live / jnp.sum(t.total, axis=1, keepdims=True)
        t.rounded_near = (t.expo_near * t.factor).astype(BF)
        t.attended = dot(t.rounded_near, t.near.value, NN)

    def attend_far(t, b):
        weight = (t.expo[:, b] * t.factor).astype(BF)
        t.rounded[:, b] = weight
        t.attended = t.attended + dot(weight, value_far[b], NN)

    def slope_near(t):
        t.attended = t.attended.astype(BF)
        t.delta = jnp.sum(t.grad.astype(F32) * t.attended.astype(F32), axis=1, keepdims=True)
        t.scaled = t.factor * SCALE
        slope = t.expo_near * t.scaled * (dot(t.grad, t.near.value, NT) - t.delta)
        slope = slope.astype(BF)
        t.query_grad = dot(slope, t.near.key, NN)
        t.query_t, t.grad_t = t.query.T, t.grad.T
        t.near.key_sum = t.near.key_sum + dot(t.query_t, slope, NN)
        t.near.value_sum = t.near.value_sum + dot(t.grad_t, t.rounded_near, NN)

    def slope_far(t, b):
        slope = t.expo[:, b] * t.scaled * (dot(t.grad, value_far[b], NT) - t.delta)
        slope = slope.astype(BF)
        t.query_grad = t.query_grad + dot(slope, key_far[b], NN)
        key_sum[:, b] += dot(t.query_t, slope, NN)
        value_sum[:, b] += dot(t.grad_t, t.rounded[:, b], NN)

    def store(t):
        query_grad = t.query_grad.astype(BF)
        for a, c in enumerate(t.cols):
            own = slice(a * ROWS, (a + 1) * ROWS)
            out[t.source, :, c] = t.attended[own]
            out[t.source, :, wide + c.start : wide + c.stop] = query_grad[own]
        if t.closes and last:
            out[t.source, :, 2 * wide : 2 * wide + HD] = t.near.key_sum.T.astype(BF)
            out[t.source, :, 2 * wide + HD :] = t.near.value_sum.T.astype(BF)
        elif t.closes:
            near_out[t.source, 0] = t.near.key_sum
            near_out[t.source, 1] = t.near.value_sum

    score_near(tiles[0])
    for b in blocks:
        score_far(tiles[0], b)
    expo_near(tiles[0])
    for b in blocks:
        expo_far(tiles[0], b)
    for t, after in zip(tiles, tiles[1:] + [None]):
        attend_near(t)
        if after:
            score_near(after)
        for b in blocks:
            attend_far(t, b)
            if after:
                score_far(after, b)
        slope_near(t)
        if after:
            expo_near(after)
        for b in blocks:
            slope_far(t, b)
            if after:
                expo_far(after, b)
        store(t)

    @pl.when(step == KV_HEADS // PER_STEP - 1)
    def _():
        if last:
            for half, summed in ((slice(0, HD), key_sum), (slice(HD, 2 * HD), value_sum)):
                terms = summed[...].T.reshape(4, KV_HEADS, OWN, HD)
                far_own[:, :, half] = terms[0]
                for i in range(3):
                    far_sent[i][:, :, half] = terms[i + 1].astype(BF)
        else:
            far_out[0] = key_sum[...]
            far_out[1] = value_sum[...]


def attend(heads, first, last, prompts, rows, pair_rows, pair_lane, far, near):
    tile = min(TILE_ROWS, heads * ROWS)
    wide = 2 * heads * HD
    width_in = wide + (2 * HD if first else 0)
    width_out = wide + (2 * HD if last else 0)
    near_spec = pl.BlockSpec((PER_STEP, 2, HD, ROWS), lambda i: (i, 0, 0, 0))
    arrays = [rows, *prompts]
    specs = [pl.BlockSpec((4, PER_STEP, 32, width_in), lambda i: (0, i, 0, 0))]
    specs += [full((KV_HEADS, OWN + META, 2 * HD))] * 4
    if not first:
        arrays += [pair_rows, far, near]
        specs += [
            pl.BlockSpec((4, PER_STEP, 32, 2 * HD), lambda i: (0, i, 0, pair_lane)),
            full((2, HD, NPOS)),
            near_spec,
        ]
    shapes = [jax.ShapeDtypeStruct((KV_HEADS, ROWS, width_out), BF)]
    out_specs = [pl.BlockSpec((PER_STEP, ROWS, width_out), lambda i: (i, 0, 0))]
    if last:
        term = (KV_HEADS, OWN, 2 * HD)
        shapes += [jax.ShapeDtypeStruct(term, F32)] + [jax.ShapeDtypeStruct(term, BF)] * 3
        out_specs += [full(term)] * 4
    else:
        shapes.append(jax.ShapeDtypeStruct((2, HD, NPOS), F32))
        out_specs.append(full((2, HD, NPOS)))
        shapes.append(jax.ShapeDtypeStruct((KV_HEADS, 2, HD, ROWS), F32))
        out_specs.append(near_spec)
    return pl.pallas_call(
        functools.partial(attend_kernel, heads, first, last, tile),
        grid=(KV_HEADS // PER_STEP,),
        in_specs=specs,
        out_specs=out_specs,
        out_shape=shapes,
        scratch_shapes=[
            pltpu.VMEM((NPOS, HD), BF),
            pltpu.VMEM((NPOS, HD), BF),
            pltpu.VMEM((tile, NPOS), F32),
            pltpu.VMEM((tile, NPOS), F32),
            pltpu.VMEM((tile, NPOS), BF),
            pltpu.VMEM((tile, NPOS), BF),
            pltpu.VMEM((HD, NPOS), F32),
            pltpu.VMEM((HD, NPOS), F32),
        ],
        compiler_params=params(),
        name="attend",
    )(*arrays)


def unpack_kernel(heads, start, last, *refs):
    refs = list(refs)
    count = 4 if last else 2
    held, got, done = refs[-3:]
    outs = refs[-3 - count : -3]
    ref = refs[0]
    wide = heads * HD
    loads = [pltpu.make_async_copy(ref.at[i], held.at[i], got.at[i]) for i in range(KV_HEADS)]
    for load in loads:
        load.start()
    if last:
        place, terms = refs[1], refs[2 : 2 + KV_HEADS]
        place_terms(place, terms, outs[3])
    copies = []
    for head, load in enumerate(loads):
        at = pl.ds((head * GROUP + start) * HD, wide)
        moves = [
            (held.at[head, :, pl.ds(0, wide)], outs[0].at[:, at]),
            (held.at[head, :, pl.ds(wide, wide)], outs[1].at[:, at]),
        ]
        if last:
            for half in range(2):
                part = held.at[head, :, pl.ds(2 * wide + half * HD, HD)]
                moves.append((part, outs[2].at[:, pl.ds((half * KV_HEADS + head) * HD, HD)]))
        load.wait()
        for a, b in moves:
            copy = pltpu.make_async_copy(a, b, done.at[len(copies)])
            copy.start()
            copies.append(copy)
    for copy in copies:
        copy.wait()


def unpack(heads, start, last, array, filled, place, terms):
    anywhere = pl.BlockSpec(memory_space=pl.ANY)
    arrays = [array]
    specs = [anywhere]
    shapes = [jax.ShapeDtypeStruct((ROWS, KV_HEADS * GROUP * HD), BF)] * 2
    out_specs = [anywhere, anywhere]
    if last:
        arrays += [place, *terms]
        specs += [pl.BlockSpec(memory_space=pltpu.SMEM)] + [full((OWN, 2 * HD))] * KV_HEADS
        summed = (1, OWN, 2 * KV_HEADS * HD)
        shapes += [jax.ShapeDtypeStruct((ROWS, 2 * KV_HEADS * HD), BF)]
        shapes += [jax.ShapeDtypeStruct(summed, F32)]
        out_specs += [anywhere, full(summed)]
    aliases = {len(arrays) + i: i for i in range(len(filled))}
    arrays += filled
    specs += [anywhere] * len(filled)
    return pl.pallas_call(
        functools.partial(unpack_kernel, heads, start, last),
        grid=(1,),
        in_specs=specs,
        out_specs=out_specs,
        out_shape=shapes,
        scratch_shapes=[
            pltpu.VMEM(array.shape, BF),
            pltpu.SemaphoreType.DMA((KV_HEADS,)),
            pltpu.SemaphoreType.DMA((4 * KV_HEADS,)),
        ],
        input_output_aliases=aliases,
        compiler_params=params(),
        name="unpack",
    )(*arrays)


def add_terms_kernel(place, own, *refs):
    terms, outs = refs[:3], refs[3:]
    for slot, out in enumerate(outs):
        head = partner(place, slot, 1)
        summed = own[head]
        for term in terms:
            summed = summed + term[head].astype(F32)
        out[...] = summed.astype(out.dtype)


def add_terms(place, own, terms):
    shape = (OWN, 2 * HD)
    kinds = [F32] + [BF] * (KV_HEADS - 1)
    return pl.pallas_call(
        add_terms_kernel,
        grid=(1,),
        in_specs=[pl.BlockSpec(memory_space=pltpu.SMEM)] + [full((KV_HEADS, *shape))] * 4,
        out_specs=[full(shape)] * KV_HEADS,
        out_shape=[jax.ShapeDtypeStruct(shape, kind) for kind in kinds],
        compiler_params=params(),
        name="add_terms",
    )(place, own, *terms)


def place_terms(place, terms, out):
    for slot, term in enumerate(terms):
        head = partner(place, slot, -1)
        key_at = pl.ds(pl.multiple_of(head * HD, HD), HD)
        value_at = pl.ds(pl.multiple_of((KV_HEADS + head) * HD, HD), HD)
        out[0, :, key_at] = term[:, :HD].astype(F32)
        out[0, :, value_at] = term[:, HD:].astype(F32)


def exchange(array, axes):
    return lax.all_to_all(array, axes, split_axis=0, concat_axis=0, tiled=True)


def shift_x(array, by):
    return lax.ppermute(array, "x", [(i, (i + by) % 4) for i in range(4)])


def shift_head(array, slot):
    pairs = []
    for yl in range(2):
        for z in range(4):
            there = ((yl + slot // 4) % 2) * 4 + (z + slot % 4) % 4
            pairs.append((yl * 4 + z, there))
    return lax.ppermute(array, ("yl", "z"), pairs)


def shift_heads(pieces):
    return [pieces[0]] + [shift_head(pieces[k], k) for k in range(1, KV_HEADS)]


def per_device(roll_query, roll_keyval, roll_grad, prompt_keyval, lengths, send_rows, land_rows):
    place = jnp.stack([lax.axis_index("yl"), lax.axis_index("z")]).astype(jnp.int32)
    prompt = exchange(pack_prompt(prompt_keyval[0], land_rows, lengths), ("yl", "z"))
    rows = []
    start = 0
    for heads in CHUNKS:
        rows.append(pack_rows(heads, start, start == 0, roll_query, roll_grad, roll_keyval, send_rows))
        start += heads
    rows[0], prompt = lax.optimization_barrier((rows[0], prompt))
    prompts = [prompt] + [shift_x(prompt, i) for i in range(1, 4)]
    received = []
    for packed in rows:
        if len(received) == 1:
            packed, prompts, received = lax.optimization_barrier((packed, prompts, received))
        packed = exchange(packed.reshape(32, 32, -1), ("grp", "yl", "z"))
        received.append(packed.reshape(4, KV_HEADS, 32, -1))
    returned = []
    carried = (None, None)
    for index, heads in enumerate(CHUNKS):
        last = index == len(CHUNKS) - 1
        results = attend(
            heads, index == 0, last, prompts, received[index], received[0], CHUNKS[0], *carried
        )
        carried = results[1:]
        if returned:
            results, earlier = lax.optimization_barrier((results, returned[-1]))
            returned[-1] = earlier
            carried = results[1:]
        returned.append(exchange(results[0], ("yl", "z")))
    sent = [shift_x(carried[i], -i) for i in range(1, 4)]
    filled = unpack(CHUNKS[0], 0, False, returned[0], (), place, ())
    sent, filled = lax.optimization_barrier((sent, filled))
    terms = shift_heads(add_terms(place, carried[0], sent))
    return tuple(unpack(CHUNKS[1], CHUNKS[0], True, returned[1], filled, place, terms))


def solution(mesh):
    mesh = Mesh(mesh.devices.reshape(4, 2, 4, 4), ("grp", "yl", "z", "x"))
    rows = P(("grp", "yl", "z", "x"), None)
    placed = P("grp", ("yl", "z", "x"), None)
    return jax.shard_map(
        per_device,
        mesh=mesh,
        in_specs=(rows, rows, rows, placed, P("grp", ("yl", "z", "x")), placed, placed),
        out_specs=(rows, rows, rows, placed),
        check_vma=False,
    )
```

```python
import functools
import math

import jax
import jax.numpy as jnp
from jax import lax
from jax.experimental import pallas as pl
from jax.experimental.pallas import tpu as pltpu
from jax.sharding import Mesh, PartitionSpec as P

KV_HEADS = 8
GROUP = 8
HD = 128
ROWS = 128
RESP_LEN = 64
NPOS = 2048
OWN = 64
META = 16
SCALE = 1.0 / math.sqrt(HD)
EXP_SCALE = SCALE * math.log2(math.e)
F32 = jnp.float32
BF = jnp.bfloat16
NN = ((1,), (0,))
NT = ((1,), (1,))

CHUNKS = (4, 4)
TILE_ROWS = 512
POS_BLOCK = 1024
PER_STEP = 4
VMEM = 65408 * 1024


def dot(a, b, dims):
    return lax.dot_general(a, b, (dims, ((), ())), preferred_element_type=F32)


def full(shape):
    return pl.BlockSpec(shape, lambda i: (0,) * len(shape))


def params():
    return pltpu.CompilerParams(dimension_semantics=("arbitrary",), vmem_limit_bytes=VMEM)


def one_hot_rows(picks):
    chosen = lax.broadcasted_iota(jnp.int32, (ROWS, ROWS), 0) == picks
    return jnp.transpose(chosen.astype(F32)).astype(BF)


def partner(place, slot, sign):
    turn = (place[1] + sign * (slot % 4) + 4) % 4
    return ((place[0] + slot // 4) % 2) * 4 + turn


def pack_prompt_kernel(prompt, land, lens, out):
    lane = lax.broadcasted_iota(jnp.int32, (META, HD), 1)
    counts = jnp.where(lane == 0, lens[:, 0:1], lens[:, 1:2]).astype(F32).astype(BF)
    rows = jnp.broadcast_to(land[0], (META, HD)).astype(F32).astype(BF)
    for head in range(KV_HEADS):
        value_at = (KV_HEADS + head) * HD
        out[head, :OWN, :HD] = prompt[:, head * HD : (head + 1) * HD]
        out[head, :OWN, HD:] = prompt[:, value_at : value_at + HD]
        out[head, OWN:, :HD] = rows
        out[head, OWN:, HD:] = counts


def pack_prompt(prompt, land, lens):
    shape = (KV_HEADS, OWN + META, 2 * HD)
    return pl.pallas_call(
        pack_prompt_kernel,
        grid=(1,),
        in_specs=[full((OWN, 2 * KV_HEADS * HD)), full((1, 1, ROWS)), full((1, 2))],
        out_specs=full(shape),
        out_shape=jax.ShapeDtypeStruct(shape, BF),
        compiler_params=params(),
        name="pack_prompt",
    )(prompt, land, lens)


def pack_rows_kernel(wide, per_step, send, *refs):
    out = refs[-1]
    order = one_hot_rows(send[0])
    for a in range(per_step):
        for ref, at in zip((refs[a], refs[per_step + a]), (0, wide)):
            moved = dot(order, ref[...], NN).astype(BF)
            out[:, a, :, at : at + wide] = moved.reshape(4, 32, wide)
        for ref, at in zip(refs[2 * per_step : -1], (2 * wide, 2 * wide + HD)):
            moved = dot(order, ref[:, a * HD : (a + 1) * HD], NN).astype(BF)
            out[:, a, :, at : at + HD] = moved.reshape(4, 32, HD)


def pack_rows(heads, start, with_pair, query, grad, pair, send):
    wide = heads * HD
    per = GROUP // heads
    first = start // heads
    per_step = 4
    steps = KV_HEADS // per_step
    specs = [full((1, 1, ROWS))]
    for _ in range(2):
        for a in range(per_step):
            specs.append(pl.BlockSpec((ROWS, wide), lambda i, a=a: (0, (i * per_step + a) * per + first)))
    arrays = [send] + [query] * per_step + [grad] * per_step
    width = 2 * wide
    if with_pair:
        specs += [
            pl.BlockSpec((ROWS, per_step * HD), lambda i: (0, i)),
            pl.BlockSpec((ROWS, per_step * HD), lambda i: (0, steps + i)),
        ]
        arrays += [pair, pair]
        width += 2 * HD
    return pl.pallas_call(
        functools.partial(pack_rows_kernel, wide, per_step),
        grid=(steps,),
        in_specs=specs,
        out_specs=pl.BlockSpec((4, per_step, 32, width), lambda i: (0, i, 0, 0)),
        out_shape=jax.ShapeDtypeStruct((4, KV_HEADS, 32, width), BF),
        compiler_params=params(),
        name="pack_rows",
    )(*arrays)


def attend_kernel(heads, first, last, tile, *refs):
    refs = list(refs)
    rows_ref, prompts = refs[0], refs[1:5]
    refs = refs[5:]
    if not first:
        pair_ref, far_in, near_in = refs[:3]
        refs = refs[3:]
    out = refs[0]
    if last:
        far_own, far_sent = refs[1], refs[2:5]
        refs = refs[5:]
    else:
        far_out, near_out = refs[1:3]
        refs = refs[3:]
    key_far, value_far, expo_even, expo_odd, rounded_even, rounded_odd, key_sum, value_sum = refs
    step = pl.program_id(0)
    wide = heads * HD
    held = KV_HEADS * OWN
    per = tile // ROWS
    parts = heads // per
    blocks = [slice(b, b + POS_BLOCK) for b in range(0, NPOS, POS_BLOCK)]
    lanes = [slice(j, j + HD) for j in range(0, POS_BLOCK, HD)]

    @pl.when(step == 0)
    def _():
        for i, prompt in enumerate(prompts):
            key_far[i * held : (i + 1) * held] = prompt[:, :OWN, :HD].reshape(held, HD)
            value_far[i * held : (i + 1) * held] = prompt[:, :OWN, HD:].reshape(held, HD)
        if first:
            key_sum[...] = jnp.zeros_like(key_sum)
            value_sum[...] = jnp.zeros_like(value_sum)
        else:
            key_sum[...] = far_in[0]
            value_sum[...] = far_in[1]

    row = lax.broadcasted_iota(jnp.int32, (ROWS, 1), 0)
    at = lax.broadcasted_iota(jnp.int32, (ROWS, ROWS), 0)
    of = lax.broadcasted_iota(jnp.int32, (ROWS, ROWS), 1)
    seen = (of <= at) & ((of // RESP_LEN) == (at // RESP_LEN))
    hide = jnp.concatenate([jnp.where(seen, 0.0, -1e30).astype(F32)] * per, 0)

    class Tile:
        pass

    tiles = []
    for source in range(PER_STEP):
        meta = prompts[0][step * PER_STEP + source, OWN:, :].astype(F32)
        order = one_hot_rows(meta[0:1, :HD].astype(jnp.int32))
        moved = dot(order, rows_ref[:, source].reshape(ROWS, -1), NN).astype(BF)
        if first:
            pair = moved[:, 2 * wide :]
        else:
            pair = dot(order, pair_ref[:, source].reshape(ROWS, -1), NN).astype(BF)
        count = jnp.where(
            row < RESP_LEN, meta[0:1, HD : HD + 1], meta[0:1, HD + 1 : HD + 2] + RESP_LEN
        )
        live = jnp.concatenate([(row.astype(F32) < count).astype(F32)] * per, 0)
        near = Tile()
        near.key, near.value = pair[:, :HD], pair[:, HD:]
        near.key_sum = jnp.zeros((HD, ROWS), F32) if first else near_in[source, 0]
        near.value_sum = jnp.zeros((HD, ROWS), F32) if first else near_in[source, 1]
        for part in range(parts):
            t = Tile()
            t.source, t.near, t.live, t.closes = source, near, live, part == parts - 1
            t.cols = [slice((part * per + a) * HD, (part * per + a + 1) * HD) for a in range(per)]
            t.query = jnp.concatenate([moved[:, c] for c in t.cols], 0)
            t.grad = jnp.concatenate([moved[:, wide + c.start : wide + c.stop] for c in t.cols], 0)
            odd = len(tiles) % 2
            t.expo, t.rounded = (expo_odd, rounded_odd) if odd else (expo_even, rounded_even)
            tiles.append(t)

    def score_near(t):
        t.score_near = dot(t.query, t.near.key, NT) + hide
        t.largest = t.score_near

    def score_far(t, b):
        score = dot(t.query, key_far[b], NT)
        t.expo[:, b] = score
        for j in lanes:
            t.largest = jnp.maximum(t.largest, score[:, j])

    def expo_near(t):
        t.shift = jnp.max(t.largest, axis=1, keepdims=True) * EXP_SCALE
        t.expo_near = jnp.exp2(t.score_near * EXP_SCALE - t.shift)
        t.total = t.expo_near

    def expo_far(t, b):
        value = jnp.exp2(t.expo[:, b] * EXP_SCALE - t.shift)
        t.expo[:, b] = value
        for j in lanes:
            t.total = t.total + value[:, j]

    def attend_near(t):
        t.factor = t.live / jnp.sum(t.total, axis=1, keepdims=True)
        t.rounded_near = (t.expo_near * t.factor).astype(BF)
        t.attended = dot(t.rounded_near, t.near.value, NN)

    def attend_far(t, b):
        weight = (t.expo[:, b] * t.factor).astype(BF)
        t.rounded[:, b] = weight
        t.attended = t.attended + dot(weight, value_far[b], NN)

    def slope_near(t):
        t.attended = t.attended.astype(BF)
        t.delta = jnp.sum(t.grad.astype(F32) * t.attended.astype(F32), axis=1, keepdims=True)
        t.scaled = t.factor * SCALE
        slope = t.expo_near * t.scaled * (dot(t.grad, t.near.value, NT) - t.delta)
        slope = slope.astype(BF)
        t.query_grad = dot(slope, t.near.key, NN)
        t.query_t, t.grad_t = t.query.T, t.grad.T
        t.near.key_sum = t.near.key_sum + dot(t.query_t, slope, NN)
        t.near.value_sum = t.near.value_sum + dot(t.grad_t, t.rounded_near, NN)

    def slope_far(t, b):
        slope = t.expo[:, b] * t.scaled * (dot(t.grad, value_far[b], NT) - t.delta)
        slope = slope.astype(BF)
        t.query_grad = t.query_grad + dot(slope, key_far[b], NN)
        key_sum[:, b] += dot(t.query_t, slope, NN)
        value_sum[:, b] += dot(t.grad_t, t.rounded[:, b], NN)

    def store(t):
        query_grad = t.query_grad.astype(BF)
        for a, c in enumerate(t.cols):
            own = slice(a * ROWS, (a + 1) * ROWS)
            out[t.source, :, c] = t.attended[own]
            out[t.source, :, wide + c.start : wide + c.stop] = query_grad[own]
        if t.closes and last:
            out[t.source, :, 2 * wide : 2 * wide + HD] = t.near.key_sum.T.astype(BF)
            out[t.source, :, 2 * wide + HD :] = t.near.value_sum.T.astype(BF)
        elif t.closes:
            near_out[t.source, 0] = t.near.key_sum
            near_out[t.source, 1] = t.near.value_sum

    score_near(tiles[0])
    for b in blocks:
        score_far(tiles[0], b)
    expo_near(tiles[0])
    for b in blocks:
        expo_far(tiles[0], b)
    for t, after in zip(tiles, tiles[1:] + [None]):
        attend_near(t)
        if after:
            score_near(after)
        for b in blocks:
            attend_far(t, b)
            if after:
                score_far(after, b)
        slope_near(t)
        if after:
            expo_near(after)
        for b in blocks:
            slope_far(t, b)
            if after:
                expo_far(after, b)
        store(t)

    @pl.when(step == KV_HEADS // PER_STEP - 1)
    def _():
        if last:
            for half, summed in ((slice(0, HD), key_sum), (slice(HD, 2 * HD), value_sum)):
                terms = summed[...].T.reshape(4, KV_HEADS, OWN, HD)
                far_own[:, :, half] = terms[0]
                for i in range(3):
                    far_sent[i][:, :, half] = terms[i + 1].astype(BF)
        else:
            far_out[0] = key_sum[...]
            far_out[1] = value_sum[...]


def attend(heads, first, last, prompts, rows, pair_rows, pair_lane, far, near):
    tile = min(TILE_ROWS, heads * ROWS)
    wide = 2 * heads * HD
    width_in = wide + (2 * HD if first else 0)
    width_out = wide + (2 * HD if last else 0)
    near_spec = pl.BlockSpec((PER_STEP, 2, HD, ROWS), lambda i: (i, 0, 0, 0))
    arrays = [rows, *prompts]
    specs = [pl.BlockSpec((4, PER_STEP, 32, width_in), lambda i: (0, i, 0, 0))]
    specs += [full((KV_HEADS, OWN + META, 2 * HD))] * 4
    if not first:
        arrays += [pair_rows, far, near]
        specs += [
            pl.BlockSpec((4, PER_STEP, 32, 2 * HD), lambda i: (0, i, 0, pair_lane)),
            full((2, HD, NPOS)),
            near_spec,
        ]
    shapes = [jax.ShapeDtypeStruct((KV_HEADS, ROWS, width_out), BF)]
    out_specs = [pl.BlockSpec((PER_STEP, ROWS, width_out), lambda i: (i, 0, 0))]
    if last:
        term = (KV_HEADS, OWN, 2 * HD)
        shapes += [jax.ShapeDtypeStruct(term, F32)] + [jax.ShapeDtypeStruct(term, BF)] * 3
        out_specs += [full(term)] * 4
    else:
        shapes.append(jax.ShapeDtypeStruct((2, HD, NPOS), F32))
        out_specs.append(full((2, HD, NPOS)))
        shapes.append(jax.ShapeDtypeStruct((KV_HEADS, 2, HD, ROWS), F32))
        out_specs.append(near_spec)
    return pl.pallas_call(
        functools.partial(attend_kernel, heads, first, last, tile),
        grid=(KV_HEADS // PER_STEP,),
        in_specs=specs,
        out_specs=out_specs,
        out_shape=shapes,
        scratch_shapes=[
            pltpu.VMEM((NPOS, HD), BF),
            pltpu.VMEM((NPOS, HD), BF),
            pltpu.VMEM((tile, NPOS), F32),
            pltpu.VMEM((tile, NPOS), F32),
            pltpu.VMEM((tile, NPOS), BF),
            pltpu.VMEM((tile, NPOS), BF),
            pltpu.VMEM((HD, NPOS), F32),
            pltpu.VMEM((HD, NPOS), F32),
        ],
        compiler_params=params(),
        name="attend",
    )(*arrays)


def unpack_kernel(heads, start, with_pair, filled, ref, *refs):
    outs, (held, got, done) = refs[filled:-3], refs[-3:]
    loads = [pltpu.make_async_copy(ref.at[i], held.at[i], got.at[i]) for i in range(KV_HEADS)]
    for load in loads:
        load.start()
    wide = heads * HD
    copies = []
    for head, load in enumerate(loads):
        at = pl.ds((head * GROUP + start) * HD, wide)
        moves = [
            (held.at[head, :, pl.ds(0, wide)], outs[0].at[:, at]),
            (held.at[head, :, pl.ds(wide, wide)], outs[1].at[:, at]),
        ]
        if with_pair:
            for half in range(2):
                part = held.at[head, :, pl.ds(2 * wide + half * HD, HD)]
                moves.append((part, outs[2].at[:, pl.ds((half * KV_HEADS + head) * HD, HD)]))
        load.wait()
        for a, b in moves:
            copy = pltpu.make_async_copy(a, b, done.at[len(copies)])
            copy.start()
            copies.append(copy)
    for copy in copies:
        copy.wait()


def unpack(heads, start, with_pair, array, filled):
    shapes = [jax.ShapeDtypeStruct((ROWS, KV_HEADS * GROUP * HD), BF)] * 2
    if with_pair:
        shapes.append(jax.ShapeDtypeStruct((ROWS, 2 * KV_HEADS * HD), BF))
    return pl.pallas_call(
        functools.partial(unpack_kernel, heads, start, with_pair, len(filled)),
        grid=(1,),
        in_specs=[pl.BlockSpec(memory_space=pl.ANY)] * (1 + len(filled)),
        out_specs=[pl.BlockSpec(memory_space=pl.ANY)] * len(shapes),
        out_shape=shapes,
        scratch_shapes=[
            pltpu.VMEM(array.shape, BF),
            pltpu.SemaphoreType.DMA((KV_HEADS,)),
            pltpu.SemaphoreType.DMA((4 * KV_HEADS,)),
        ],
        input_output_aliases={1 + i: i for i in range(len(filled))},
        compiler_params=params(),
        name="unpack",
    )(array, *filled)


def add_terms_kernel(place, own, *refs):
    terms, outs = refs[:3], refs[3:]
    for slot, out in enumerate(outs):
        head = partner(place, slot, 1)
        summed = own[head]
        for term in terms:
            summed = summed + term[head].astype(F32)
        out[...] = summed.astype(out.dtype)


def add_terms(place, own, terms):
    shape = (OWN, 2 * HD)
    kinds = [F32] + [BF] * (KV_HEADS - 1)
    return pl.pallas_call(
        add_terms_kernel,
        grid=(1,),
        in_specs=[pl.BlockSpec(memory_space=pltpu.SMEM)] + [full((KV_HEADS, *shape))] * 4,
        out_specs=[full(shape)] * KV_HEADS,
        out_shape=[jax.ShapeDtypeStruct(shape, kind) for kind in kinds],
        compiler_params=params(),
        name="add_terms",
    )(place, own, *terms)


def place_terms_kernel(place, *refs):
    out = refs[-1]
    for slot, term in enumerate(refs[:-1]):
        head = partner(place, slot, -1)
        key_at = pl.ds(pl.multiple_of(head * HD, HD), HD)
        value_at = pl.ds(pl.multiple_of((KV_HEADS + head) * HD, HD), HD)
        out[0, :, key_at] = term[:, :HD].astype(F32)
        out[0, :, value_at] = term[:, HD:].astype(F32)


def place_terms(place, terms):
    shape = (1, OWN, 2 * KV_HEADS * HD)
    return pl.pallas_call(
        place_terms_kernel,
        grid=(1,),
        in_specs=[pl.BlockSpec(memory_space=pltpu.SMEM)] + [full((OWN, 2 * HD))] * KV_HEADS,
        out_specs=full(shape),
        out_shape=jax.ShapeDtypeStruct(shape, F32),
        compiler_params=params(),
        name="place_terms",
    )(place, *terms)


def exchange(array, axes):
    return lax.all_to_all(array, axes, split_axis=0, concat_axis=0, tiled=True)


def shift_x(array, by):
    return lax.ppermute(array, "x", [(i, (i + by) % 4) for i in range(4)])


def shift_head(array, slot):
    pairs = []
    for yl in range(2):
        for z in range(4):
            there = ((yl + slot // 4) % 2) * 4 + (z + slot % 4) % 4
            pairs.append((yl * 4 + z, there))
    return lax.ppermute(array, ("yl", "z"), pairs)


def shift_heads(pieces):
    return [pieces[0]] + [shift_head(pieces[k], k) for k in range(1, KV_HEADS)]


def per_device(roll_query, roll_keyval, roll_grad, prompt_keyval, lengths, send_rows, land_rows):
    place = jnp.stack([lax.axis_index("yl"), lax.axis_index("z")]).astype(jnp.int32)
    prompt = exchange(pack_prompt(prompt_keyval[0], land_rows, lengths), ("yl", "z"))
    rows = []
    start = 0
    for heads in CHUNKS:
        rows.append(pack_rows(heads, start, start == 0, roll_query, roll_grad, roll_keyval, send_rows))
        start += heads
    rows[0], prompt = lax.optimization_barrier((rows[0], prompt))
    prompts = [prompt] + [shift_x(prompt, i) for i in range(1, 4)]
    received = []
    for packed in rows:
        if len(received) == 1:
            packed, prompts, received = lax.optimization_barrier((packed, prompts, received))
        packed = exchange(packed.reshape(32, 32, -1), ("grp", "yl", "z"))
        received.append(packed.reshape(4, KV_HEADS, 32, -1))
    returned = []
    carried = (None, None)
    for index, heads in enumerate(CHUNKS):
        last = index == len(CHUNKS) - 1
        results = attend(
            heads, index == 0, last, prompts, received[index], received[0], CHUNKS[0], *carried
        )
        carried = results[1:]
        if returned:
            results, earlier = lax.optimization_barrier((results, returned[-1]))
            returned[-1] = earlier
            carried = results[1:]
        returned.append(exchange(results[0], ("yl", "z")))
    terms = [shift_x(carried[i], -i) for i in range(1, 4)]
    filled = ()
    start = 0
    for index, heads in enumerate(CHUNKS):
        last = index == len(CHUNKS) - 1
        if last:
            terms, filled = lax.optimization_barrier((terms, filled))
        filled = unpack(heads, start, last, returned[index], filled[:2])
        start += heads
    terms = shift_heads(add_terms(place, carried[0], terms))
    terms, filled = lax.optimization_barrier((terms, filled))
    return (*filled, place_terms(place, terms))


def solution(mesh):
    mesh = Mesh(mesh.devices.reshape(4, 2, 4, 4), ("grp", "yl", "z", "x"))
    rows = P(("grp", "yl", "z", "x"), None)
    placed = P("grp", ("yl", "z", "x"), None)
    return jax.shard_map(
        per_device,
        mesh=mesh,
        in_specs=(rows, rows, rows, placed, P("grp", ("yl", "z", "x")), placed, placed),
        out_specs=(rows, rows, rows, placed),
        check_vma=False,
    )
```
